128 devices in a mesh: section: 8 (over x_hi, y), dp: 16 (over z, x_lo, core).
Axes of the slice: x: 4 (x_hi: 2, x_lo: 2; x = x_hi * 2 + x_lo), y: 4, z: 4, core: 2. Of those that a mesh axis runs over, the one named last changes fastest.
Arguments:
- state: bfloat16 [8, 256, 3072], P(None, 'dp'), may hold values from -17 to 17
- adjoint: bfloat16 [8, 256, 3072], P(None, 'dp'), may hold values from -6 to 6
- probe: int32 [8, 256, 3072], P(None, 'dp'), may hold values from -1 to 1, as said below
- logp: float32 [8, 16], P(None, 'dp'), may hold values from -6 to 6
- density_weight: float32 [8, 16], P(None, 'dp'), may hold values from 0.5 to 1.5
- step_size: float32 [1], replicated, may hold values from 0.2 to 0.5
- norm_gain: float32 [8, 3072], P('section'), may hold values from 0.25 to 1.75
- norm_shift: float32 [8, 3072], P('section'), may hold values from -3 to 3
- branch_gate: float32 [8, 3072], P('section'), may hold values from 0.4 to 1.2
- weights: bfloat16 [8, 3072, 3072], P('section'), may hold values from -1 to 1
Outputs:
- state_next: float32 [8, 256, 3072], P('section', 'dp')
- adjoint_next: float32 [8, 256, 3072], P('section', 'dp')
- logp_next: float32 [8, 16], P('section', 'dp')
- weight_grad: float32 [8, 3072, 3072], P('section', 'dp')
The draws below stay inside these ranges and needn't reach their ends.
Inputs may be any that keep to these rules, and one draw needn't show every extreme that they name: `probe`: every entry is -1 or +1.
All inputs are finite; a program needn't handle non-finite values.
Results may differ from the reference program's by a relative error of at most 0.022.
Values may be sent and summed in bfloat16 or wider, within the bound.
A program may use at most 192 MiB of HBM per device.

```python
import math
import jax
import jax.numpy as jnp
from jax import lax

D = 3072
TOK_DEV = 16
LAYERS = 8
MICRO = 8
IMAGES = 16
ROWS = 256


def draw_state(key, part):
    key = jax.random.fold_in(key, 11)
    key_base, key_rows, key_cols = jax.random.split(key, 3)
    array_shape = (MICRO, ROWS, D)
    row_scale = jnp.exp(jax.random.uniform(key_rows, (MICRO, ROWS, 1), jnp.float32, math.log(0.3), math.log(3.0)))
    col_scale = jnp.exp(jax.random.uniform(key_cols, (1, 1, D), jnp.float32, math.log(0.5), math.log(1.6)))
    base_draw = jax.random.truncated_normal(key_base, -3.5, 3.5, array_shape, jnp.float32)
    return (base_draw * row_scale * col_scale).astype(jnp.bfloat16)


def draw_probe(key, part):
    key = jax.random.fold_in(key, 23)
    coin_flips = jax.random.randint(key, (MICRO, ROWS, D), 0, 2)
    return (coin_flips * 2 - 1).astype(jnp.int32)


def draw_weights(key, part):
    key = jax.random.fold_in(key, 41)
    array_shape = (LAYERS, D, D)
    noise_draw = jax.random.truncated_normal(key, -3.0, 3.0, array_shape, jnp.float32)
    row_ids = lax.broadcasted_iota(jnp.int32, array_shape, 1)
    col_ids = lax.broadcasted_iota(jnp.int32, array_shape, 2)
    identity = (row_ids == col_ids).astype(jnp.float32)
    return (0.6 * identity + noise_draw * D ** (-0.5)).astype(jnp.bfloat16)


def level_of(key, dims, cuts, low, largest):
    loudness = 1.0
    for axis_at, shards_of in cuts:
        steps = jax.random.uniform(jax.random.fold_in(jax.random.fold_in(key, 6), axis_at), (shards_of,), jnp.float32, low / len(cuts), largest / len(cuts))
        loudness = loudness * jnp.repeat(jnp.exp(steps), dims[axis_at] // shards_of).reshape((-1,) + (1,) * (len(dims) - 1 - axis_at))
    return loudness


def normal_values(rng, dims, deviation, reach, cuts=(), kind=jnp.bfloat16):
    loudness = level_of(rng, dims, cuts, -0.22, 0.18) if cuts else 1.0
    values = jax.random.normal(rng, dims, jnp.float32) * deviation * loudness
    return jnp.minimum(jnp.maximum(values, -reach), reach).astype(kind)


def setup_inputs(seed: int = 0) -> dict:
    splits = jax.random.split(jax.random.key(seed), 11)
    state = draw_state(jax.random.fold_in(splits[10], 71), 0)
    adjoint = normal_values(splits[1], (MICRO, ROWS, D), 1.0, 6.0, ((1, 16),))
    probe = draw_probe(jax.random.fold_in(splits[10], 71), 0)
    logp = normal_values(splits[3], (MICRO, IMAGES), 1.0, 6.0, ((1, 16),), jnp.float32)
    density_weight = jnp.clip(0.5 + 1.0 * jax.random.uniform(splits[4], (MICRO, IMAGES), jnp.float32) ** level_of(splits[4], (MICRO, IMAGES), ((1, 16),), -0.2, 0.2), 0.5, 1.5)
    step_size = jnp.clip(jax.random.uniform(splits[5], (1,), jnp.float32, 0.2, 0.5), 0.2, 0.5)
    norm_gain = jnp.clip(1.0 + 0.15 * jax.random.normal(splits[6], (LAYERS, D), jnp.float32), 0.25, 1.75)
    norm_shift = normal_values(splits[7], (LAYERS, D), 0.5, 3.0, ((0, 8),), jnp.float32)
    branch_gate = jnp.clip(0.4 + 0.800000042 * jax.random.uniform(splits[8], (LAYERS, D), jnp.float32) ** level_of(splits[8], (LAYERS, D), ((0, 8),), -0.2, 0.2), 0.4, 1.2)
    weights = draw_weights(jax.random.fold_in(splits[10], 71), 0)
    return {"state": state, "adjoint": adjoint, "probe": probe, "logp": logp, "density_weight": density_weight, "step_size": step_size, "norm_gain": norm_gain, "norm_shift": norm_shift, "branch_gate": branch_gate, "weights": weights}


EPSILON = 1e-06

def normalize(gain_row, shift_row):

    def mapped(values):
        center = lax.optimization_barrier(jnp.mean(values, axis=-1, keepdims=True))
        centered = values - center
        spread = lax.optimization_barrier(jnp.mean(centered * centered, axis=-1, keepdims=True))
        return centered * lax.rsqrt(spread + EPSILON) * gain_row + shift_row
    return mapped

def gated_gelu(gate_row):

    def mapped(values):
        return gate_row * jax.nn.gelu(values, approximate=False)
    return mapped

def layer_forward(rows_in, tangent_in, gain_row, shift_row, gate_row, weight_mat):
    base_rows = rows_in.astype(jnp.float32)
    tangent_rows = tangent_in.astype(jnp.float32)
    normed, normed_t = jax.jvp(normalize(gain_row, shift_row), (base_rows,), (tangent_rows,))
    normed_pair = jnp.concatenate([normed, normed_t], axis=0).astype(jnp.bfloat16)
    products = jnp.dot(normed_pair, weight_mat, preferred_element_type=jnp.float32)
    row_total = rows_in.shape[0]
    branch, branch_t = jax.jvp(gated_gelu(gate_row), (products[:row_total],), (products[row_total:],))
    return (base_rows + branch, tangent_rows + branch_t, normed_pair, products)

def layer_backward(rows_in, tangent_in, cotangent, cotangent_t, gain_row, shift_row, gate_row, weight_mat, products):
    row_total = rows_in.shape[0]

    def branch_pair(values, values_t):
        return jax.jvp(gated_gelu(gate_row), (values,), (values_t,))
    _, pull_back = jax.vjp(branch_pair, products[:row_total], products[row_total:])
    grad_z, grad_zt = pull_back((cotangent, cotangent_t))
    grad_pair = jnp.concatenate([grad_z, grad_zt], axis=0).astype(jnp.bfloat16)
    grad_normed = lax.dot_general(grad_pair, weight_mat, (((1,), (1,)), ((), ())), preferred_element_type=jnp.float32)

    def norm_pair(values, values_t):
        return jax.jvp(normalize(gain_row, shift_row), (values,), (values_t,))
    _, pull_norm = jax.vjp(norm_pair, rows_in.astype(jnp.float32), tangent_in.astype(jnp.float32))
    grad_rows, grad_tangent = pull_norm((grad_normed[:row_total], grad_normed[row_total:]))
    return (cotangent + grad_rows, cotangent_t + grad_tangent, grad_pair)

def by_position(pair_rows):
    shaped = pair_rows.reshape(2, MICRO, IMAGES, TOK_DEV, D)
    return shaped.transpose(2, 0, 1, 3, 4).reshape(IMAGES, 2 * MICRO * TOK_DEV, D)

def shard_sums(normed_pair, grad_pair):

    def add_position(running_sum, pieces):
        partial_sum = jnp.dot(pieces[0].T, pieces[1], preferred_element_type=jnp.float32)
        rounded = lax.optimization_barrier(partial_sum.astype(jnp.bfloat16))
        return (running_sum + rounded.astype(jnp.float32), None)
    start_sum = jnp.zeros((D, D), jnp.float32)
    result, _ = lax.scan(add_position, start_sum, (by_position(normed_pair), by_position(grad_pair)))
    return result

def reference(state, adjoint, probe, logp, density_weight, step_size, norm_gain, norm_shift, branch_gate, weights):
    total_rows = MICRO * ROWS
    rows_now = state.reshape(total_rows, D)
    sign_rows = probe.reshape(total_rows, D).astype(jnp.float32)
    tangent_now = probe.reshape(total_rows, D).astype(jnp.bfloat16)
    saved_inputs = []
    for layer_index in range(LAYERS):
        saved_inputs.append((rows_now, tangent_now))
        out_rows, out_tangent, _, _ = layer_forward(rows_now, tangent_now, norm_gain[layer_index], norm_shift[layer_index], branch_gate[layer_index], weights[layer_index])
        rows_now = lax.optimization_barrier(out_rows.astype(jnp.bfloat16))
        tangent_now = lax.optimization_barrier(out_tangent.astype(jnp.bfloat16))
    weight_per_row = jnp.repeat(density_weight, TOK_DEV, axis=1).reshape(total_rows, 1)
    cotangent = adjoint.reshape(total_rows, D).astype(jnp.float32)
    cotangent_t = -weight_per_row * sign_rows
    grad_list = []
    for layer_index in reversed(range(LAYERS)):
        base_rows, base_tangent = saved_inputs[layer_index]
        _, _, normed_pair, products = layer_forward(base_rows, base_tangent, norm_gain[layer_index], norm_shift[layer_index], branch_gate[layer_index], weights[layer_index])
        back_rows, back_tangent, grad_pair = layer_backward(base_rows, base_tangent, cotangent, cotangent_t, norm_gain[layer_index], norm_shift[layer_index], branch_gate[layer_index], weights[layer_index], products)
        grad_list.append(shard_sums(normed_pair, grad_pair))
        cotangent = lax.optimization_barrier(back_rows.astype(jnp.bfloat16)).astype(jnp.float32)
        cotangent_t = lax.optimization_barrier(back_tangent.astype(jnp.bfloat16)).astype(jnp.float32)
    weight_grad = jnp.stack(grad_list[::-1])
    step_value = step_size[0]
    start_rows = state.astype(jnp.float32)
    final_rows = rows_now.reshape(MICRO, ROWS, D).astype(jnp.float32)
    state_next = start_rows - step_value * (final_rows - start_rows)
    final_tangent = tangent_now.astype(jnp.float32)
    entry_terms = (sign_rows * (final_tangent - sign_rows)).reshape(MICRO, IMAGES, TOK_DEV * D)
    divergence = lax.optimization_barrier(jnp.sum(entry_terms, axis=-1)) / (TOK_DEV * D)
    logp_next = logp + step_value * divergence
    adjoint_rows = adjoint.astype(jnp.float32)
    adjoint_next = adjoint_rows + step_value * (cotangent.reshape(MICRO, ROWS, D) - adjoint_rows)
    return (state_next, adjoint_next, logp_next, weight_grad)
```

```python
import functools

import jax
import jax.numpy as jnp
from jax import lax
from jax.experimental import pallas as pl
from jax.experimental.pallas import tpu as pltpu
from jax.sharding import PartitionSpec as P

EPSILON = 1e-06
MESH = pl.DeviceIdType.MESH
CHUNKS = 4
ROOT_HALF = 0.7071067811865476
PHI_SCALE = 0.3989422804014327
F32 = jnp.float32
BF16 = jnp.bfloat16


def wait_bytes(ref, sem):
    pltpu.make_async_copy(ref, ref, sem).wait()


def lanes(value):
    total = value[:, 0:128]
    for at in range(128, value.shape[1], 128):
        total = total + value[:, at : at + 128]
    return total


def kernel(
    sections, dp_size, tok, feat,
    xs_hbm, cs_hbm, dw_hbm, gain_ref, shift_ref, gate_ref, w_hbm,
    fin_u, fin_b, fin_div, grad_out,
    w_vm, wt_vm, x_in, out_buf, c_in, n_buf, n_loc, g_loc, n_all, g_all,
    g1_buf, g2_buf, ab_buf, stats, scale, div_buf, ex_recv,
    w_sem, in_sem, x_ssem, x_rsem, c_ssem, c_rsem, n_ssem, n_rsem, g_ssem, g_rsem,
    fu_rsem, fb_rsem, dv_ssem, dv_rsem, sc_ssem, sc_rsem, e_ssem, e_rsem, f_ssem, f_rsem,
):
    micros = sections
    cw = feat // CHUNKS
    pair = 2 * tok
    chips = dp_size // 2
    halves = chips // 4
    ncols = feat // halves
    keep = ncols // 2
    piece = keep // 4
    tile = 256
    inv = 1.0 / feat
    half_section = sections // 2
    last = sections - 1

    s = lax.axis_index("section")
    d = lax.axis_index("dp")
    core = lax.rem(d, 2)
    chip = lax.div(d, 2)
    x_at = lax.rem(chip, 2)
    d_flip = d + 2 - 4 * x_at
    z_at = lax.div(chip, 2)
    my_half = lax.div(chip, 4)
    my_col = lax.rem(chip, 4)
    next_d = jnp.where(s == half_section - 1, d_flip, d)
    prev_d = jnp.where(s == half_section, d_flip, d)

    def w_copy(k):
        cols = pl.ds(k * cw, cw)
        return pltpu.make_async_copy(w_hbm.at[:, cols], w_vm.at[:, cols], w_sem.at[k])

    for k in range(CHUNKS):
        w_copy(k).start()

    def x_copy(m):
        return pltpu.make_async_copy(xs_hbm.at[m], x_in.at[m], in_sem.at[m])

    @pl.when(s == 0)
    def _():
        for m in range(micros):
            x_copy(m).start()

    barrier = pltpu.get_barrier_semaphore()

    def greet_group(i, carry):
        other = lax.rem(d + i, dp_size)
        pl.semaphore_signal(barrier, inc=1, device_id=(s, other), device_id_type=MESH)
        return carry

    def greet_sections(i, carry):
        other = lax.rem(s + i, sections)
        pl.semaphore_signal(barrier, inc=1, device_id=(other, d), device_id_type=MESH)
        pl.semaphore_signal(barrier, inc=1, device_id=(other, d_flip), device_id_type=MESH)
        return carry

    lax.fori_loop(1, dp_size, greet_group, 0)
    lax.fori_loop(1, sections, greet_sections, 0)
    pl.semaphore_wait(barrier, dp_size - 1 + 2 * (sections - 1))

    def seed_copy(m):
        return pltpu.make_async_remote_copy(
            src_ref=cs_hbm.at[m],
            dst_ref=c_in.at[m],
            send_sem=c_ssem.at[m, 0],
            recv_sem=c_rsem.at[m, 0],
            device_id=(s, d_flip),
            device_id_type=MESH,
        )

    def scale_copy():
        return pltpu.make_async_remote_copy(
            src_ref=dw_hbm,
            dst_ref=scale,
            send_sem=sc_ssem,
            recv_sem=sc_rsem,
            device_id=(s, d_flip),
            device_id_type=MESH,
        )

    @pl.when(s == last)
    def _():
        scale_copy().start()
        for m in range(micros):
            seed_copy(m).start()

    @pl.when(s != last)
    def _():
        scale[...] = jnp.ones_like(scale)

    def transpose_weights():
        count = feat // tile

        def one(i, carry):
            at_row = pl.multiple_of(lax.div(i, count) * tile, tile)
            at_col = pl.multiple_of(lax.rem(i, count) * tile, tile)
            wt_vm[pl.ds(at_col, tile), pl.ds(at_row, tile)] = w_vm[
                pl.ds(at_row, tile), pl.ds(at_col, tile)
            ].T
            return carry

        lax.fori_loop(0, count * count, one, 0)

    @pl.when(s >= half_section)
    def _():
        for k in range(CHUNKS):
            w_copy(k).wait()
        transpose_weights()

    def x_send(m, k):
        return pltpu.make_async_remote_copy(
            src_ref=out_buf.at[m, k],
            dst_ref=x_in.at[m, k],
            send_sem=x_ssem.at[m, k],
            recv_sem=x_rsem.at[m, k],
            device_id=(s + 1, next_d),
            device_id_type=MESH,
        )

    def top_send(m, k):
        return pltpu.make_async_remote_copy(
            src_ref=out_buf.at[m, k, pl.ds(0, tok)],
            dst_ref=fin_u.at[k],
            send_sem=x_ssem.at[m, k],
            recv_sem=fu_rsem.at[k],
            device_id=(m, d_flip),
            device_id_type=MESH,
        )

    def gather_send(loc, everything, ssem, rsem, m, index, other):
        return pltpu.make_async_remote_copy(
            src_ref=loc.at[m, index],
            dst_ref=everything.at[m, chip],
            send_sem=ssem.at[m],
            recv_sem=rsem.at[m],
            device_id=(s, other * 2 + core),
            device_id_type=MESH,
        )

    def forward(m, carry):
        @pl.when(s == 0)
        def _():
            x_copy(m).wait()

        @pl.when(s > 0)
        def _():
            for k in range(CHUNKS):
                wait_bytes(x_in.at[m, k], x_rsem.at[m, k])

        def rows(k):
            return x_in[m, k, pl.ds(0, tok), :].astype(F32)

        def tangents(k):
            return x_in[m, k, pl.ds(tok, tok), :].astype(F32)

        total_u = total_w = 0.0
        for k in range(CHUNKS):
            total_u = total_u + lanes(rows(k))
            total_w = total_w + lanes(tangents(k))
        mean_u = jnp.sum(total_u, axis=1, keepdims=True) * inv
        mean_w = jnp.sum(total_w, axis=1, keepdims=True) * inv
        square = cross = 0.0
        for k in range(CHUNKS):
            centered = rows(k) - mean_u
            square = square + lanes(centered * centered)
            cross = cross + lanes(centered * (tangents(k) - mean_w))
        var = jnp.sum(square, axis=1, keepdims=True) * inv
        cov = jnp.sum(cross, axis=1, keepdims=True) * inv
        rinv = lax.rsqrt(var + EPSILON)
        slope = rinv * cov
        for at, value in enumerate((mean_u, mean_w, rinv, slope)):
            stats[m, at] = jnp.broadcast_to(value, (tok, 128))
        for k in range(CHUNKS):
            cols = pl.ds(k * cw, cw)
            gain = gain_ref[:, cols]
            xhat = (rows(k) - mean_u) * rinv
            normed = xhat * gain + shift_ref[:, cols]
            normed_t = rinv * ((tangents(k) - mean_w) - xhat * slope) * gain
            n_buf[pl.ds(0, tok), cols] = normed.astype(BF16)
            n_buf[pl.ds(tok, tok), cols] = normed_t.astype(BF16)
        for at in range(halves):
            n_loc[m, at] = n_buf[:, pl.ds(at * ncols, ncols)]

        def send_n(i, carry):
            other = lax.rem(chip + i, chips)
            gather_send(n_loc, n_all, n_ssem, n_rsem, m, lax.div(other, 4), other).start()
            return carry

        lax.fori_loop(1, chips, send_n, 0)
        n_all[m, chip] = n_loc[m, my_half]

        for k in range(CHUNKS):
            cols = pl.ds(k * cw, cw)

            @pl.when((m == 0) & (s < half_section))
            def _():
                w_copy(k).wait()

            product = jnp.dot(n_buf[...], w_vm[:, cols], preferred_element_type=F32)
            z = product[:tok]
            z_t = product[tok:]
            gate = gate_ref[:, cols]
            cdf = 0.5 + 0.5 * lax.erf(z * ROOT_HALF)
            zz = z * z
            pdf = PHI_SCALE * jnp.exp(-0.5 * zz)
            first = gate * (cdf + z * pdf)
            out_buf[m, k, pl.ds(0, tok), :] = (rows(k) + gate * (z * cdf)).astype(BF16)
            out_buf[m, k, pl.ds(tok, tok), :] = (tangents(k) + first * z_t).astype(BF16)

            @pl.when(s < last)
            def _():
                x_send(m, k).start()

            @pl.when(s == last)
            def _():
                top_send(m, k).start()

            g1_buf[m, k] = first
            g2_buf[m, k] = gate * (pdf * (2.0 - zz)) * z_t
        return carry

    lax.fori_loop(0, micros, forward, 0)

    @pl.when(s < half_section)
    def _():
        transpose_weights()

    @pl.when(s == last)
    def _():
        wait_bytes(scale, sc_rsem)
        scale_copy().wait_send()
        for m in range(micros):
            seed_copy(m).wait_send()

    def c_send(m, k):
        return pltpu.make_async_remote_copy(
            src_ref=out_buf.at[m, k],
            dst_ref=c_in.at[m, k],
            send_sem=c_ssem.at[m, k],
            recv_sem=c_rsem.at[m, k],
            device_id=(s - 1, prev_d),
            device_id_type=MESH,
        )

    def back_send(m, k):
        return pltpu.make_async_remote_copy(
            src_ref=out_buf.at[m, k, pl.ds(0, tok)],
            dst_ref=fin_b.at[k],
            send_sem=c_ssem.at[m, k],
            recv_sem=fb_rsem.at[k],
            device_id=(m, d),
            device_id_type=MESH,
        )

    def back_own(k):
        return pltpu.make_async_copy(
            out_buf.at[0, k, pl.ds(0, tok)], fin_b.at[k], fb_rsem.at[k]
        )

    def div_send(m):
        return pltpu.make_async_remote_copy(
            src_ref=div_buf.at[m],
            dst_ref=fin_div,
            send_sem=dv_ssem.at[m],
            recv_sem=dv_rsem,
            device_id=(m, d_flip),
            device_id_type=MESH,
        )

    def backward(m, carry):
        @pl.when(s == last)
        def _():
            wait_bytes(c_in.at[m], c_rsem.at[m, 0])
            total = 0.0
            for k in range(CHUNKS):
                sign = c_in[m, k, pl.ds(tok, tok), :].astype(F32)
                top = out_buf[m, k, pl.ds(tok, tok), :].astype(F32)
                total = total + lanes(sign * (top - sign))
            div_buf[m] = total[:8] + total[8:]
            div_send(m).start()
            for k in range(CHUNKS):
                top_send(m, k).wait_send()

        @pl.when(s < last)
        def _():
            for k in range(CHUNKS):
                wait_bytes(c_in.at[m, k], c_rsem.at[m, k])
                x_send(m, k).wait_send()

        factor = scale[m, 0:1, 0:1]

        def cot(k):
            return c_in[m, k, pl.ds(0, tok), :].astype(F32)

        def cot_t(k):
            return c_in[m, k, pl.ds(tok, tok), :].astype(F32) * factor

        for k in range(CHUNKS):
            cols = pl.ds(k * cw, cw)
            first = g1_buf[m, k]
            c_t = cot_t(k)
            top = (cot(k) * first + c_t * g2_buf[m, k]).astype(BF16)
            low = (c_t * first).astype(BF16)
            n_buf[pl.ds(0, tok), cols] = top
            n_buf[pl.ds(tok, tok), cols] = low
            g_loc[m, k, pl.ds(0, tok), :] = top
            g_loc[m, k, pl.ds(tok, tok), :] = low

        def send_g(i, carry):
            other = lax.rem(chip + i, chips)
            gather_send(g_loc, g_all, g_ssem, g_rsem, m, lax.rem(other, 4), other).start()
            return carry

        lax.fori_loop(1, chips, send_g, 0)
        g_all[m, chip] = g_loc[m, my_col]

        mean_u = stats[m, 0][:, 0:1]
        mean_w = stats[m, 1][:, 0:1]
        rinv = stats[m, 2][:, 0:1]
        slope = stats[m, 3][:, 0:1]

        def hat(k):
            return (x_in[m, k, pl.ds(0, tok), :].astype(F32) - mean_u) * rinv

        def centered_w(k):
            return x_in[m, k, pl.ds(tok, tok), :].astype(F32) - mean_w

        sums = [0.0] * 5
        for k in range(CHUNKS):
            cols = pl.ds(k * cw, cw)
            product = jnp.dot(n_buf[...], wt_vm[:, cols], preferred_element_type=F32)
            gain = gain_ref[:, cols]
            a = product[:tok] * gain
            b = product[tok:] * gain
            ab_buf[k, pl.ds(0, tok), :] = a
            ab_buf[k, pl.ds(tok, tok), :] = b
            xhat = hat(k)
            for at, value in enumerate((a, a * xhat, b, b * xhat, b * centered_w(k))):
                sums[at] = sums[at] + lanes(value)
        mean_a, mean_ax, mean_b, mean_bx, mean_bw = (
            jnp.sum(value, axis=1, keepdims=True) * inv for value in sums
        )
        square = rinv * rinv
        for k in range(CHUNKS):
            xhat = hat(k)
            a = ab_buf[k, pl.ds(0, tok), :]
            b = ab_buf[k, pl.ds(tok, tok), :] - mean_b
            back_u = (
                cot(k)
                + rinv * (a - mean_a - xhat * mean_ax)
                - square
                * (
                    xhat * (mean_bw - 3.0 * mean_bx * slope)
                    + slope * b
                    + mean_bx * centered_w(k)
                )
            )
            back_w = cot_t(k) + rinv * (b - xhat * mean_bx)
            out_buf[m, k, pl.ds(0, tok), :] = back_u.astype(BF16)
            out_buf[m, k, pl.ds(tok, tok), :] = back_w.astype(BF16)

            @pl.when(s > 0)
            def _():
                c_send(m, k).start()

            @pl.when((s == 0) & (m > 0))
            def _():
                back_send(m, k).start()

            @pl.when((s == 0) & (m == 0))
            def _():
                back_own(k).start()

        return carry

    lax.fori_loop(0, micros, backward, 0)

    def arrived(m, carry):
        wait_bytes(n_all.at[m, pl.ds(0, chips - 1)], n_rsem.at[m])
        wait_bytes(g_all.at[m, pl.ds(0, chips - 1)], g_rsem.at[m])
        return carry

    lax.fori_loop(0, micros, arrived, 0)

    half_micros = micros // 2
    depth = half_micros * chips * pair
    tiles = keep // tile
    ex_send = w_vm.at[pl.ds(0, keep), pl.ds(0, cw)]
    fin_send = w_vm.at[pl.ds(keep, keep), pl.ds(0, cw)]

    def block(start):
        cols = pl.ds(pl.multiple_of(start, tile), tile)
        total = 0.0
        for first in (0, half_micros):
            some = pl.ds(first, half_micros)
            left = n_all[some, :, :, cols].reshape(depth, tile)
            right = g_all[some].reshape(depth, cw)
            total = total + lax.dot_general(
                left, right, (((0,), (0,)), ((), ())), preferred_element_type=F32
            )
        return total

    def ex_copy(i):
        at = pl.ds(i * tile, tile)
        return pltpu.make_async_remote_copy(
            src_ref=ex_send.at[at],
            dst_ref=ex_recv.at[at],
            send_sem=e_ssem.at[i],
            recv_sem=e_rsem.at[i],
            device_id=(s, d + 1 - 2 * core),
            device_id_type=MESH,
        )

    for i in range(tiles):
        ex_send[pl.ds(i * tile, tile), :] = block((1 - core) * keep + i * tile).astype(BF16)
        ex_copy(i).start()
    for i in range(tiles):
        at = pl.ds(i * tile, tile)
        mine = block(core * keep + i * tile)
        wait_bytes(ex_recv.at[at], e_rsem.at[i])
        fin_send[at, :] = (mine + ex_recv[at, :].astype(F32)).astype(BF16)

    goal = (2 * my_half + core) * 4

    def piece_send(j):
        return pltpu.make_async_remote_copy(
            src_ref=fin_send.at[pl.ds(j * piece, piece)],
            dst_ref=grad_out.at[my_col],
            send_sem=f_ssem.at[j],
            recv_sem=f_rsem.at[my_col],
            device_id=(s, goal + j),
            device_id_type=MESH,
        )

    def piece_own(j):
        return pltpu.make_async_copy(
            fin_send.at[pl.ds(j * piece, piece)], grad_out.at[my_col], f_rsem.at[my_col]
        )

    for j in range(4):

        @pl.when(goal + j != d)
        def _():
            piece_send(j).start()

        @pl.when(goal + j == d)
        def _():
            piece_own(j).start()

    for k in range(CHUNKS):
        wait_bytes(fin_u.at[k], fu_rsem.at[k])
        wait_bytes(fin_b.at[k], fb_rsem.at[k])
    wait_bytes(fin_div, dv_rsem)

    def drain(m, carry):
        wait_bytes(n_all.at[m, pl.ds(0, chips - 1)], n_ssem.at[m])
        wait_bytes(g_all.at[m, pl.ds(0, chips - 1)], g_ssem.at[m])

        @pl.when(s == last)
        def _():
            div_send(m).wait_send()

        @pl.when(s > 0)
        def _():
            for k in range(CHUNKS):
                c_send(m, k).wait_send()

        @pl.when((s == 0) & (m > 0))
        def _():
            for k in range(CHUNKS):
                back_send(m, k).wait_send()

        return carry

    lax.fori_loop(0, micros, drain, 0)
    for i in range(tiles):
        ex_copy(i).wait_send()
    for j in range(4):

        @pl.when(goal + j != d)
        def _():
            piece_send(j).wait_send()

        wait_bytes(grad_out.at[j], f_rsem.at[j])


def run_kernel(sections, dp_size, tok, feat, *operands):
    micros = sections
    cw = feat // CHUNKS
    pair = 2 * tok
    chips = dp_size // 2
    halves = chips // 4
    ncols = feat // halves
    keep = ncols // 2
    piece = keep // 4
    dma = pltpu.SemaphoreType.DMA
    anywhere = pl.BlockSpec(memory_space=pl.ANY)
    vmem = pl.BlockSpec(memory_space=pltpu.VMEM)
    return pl.pallas_call(
        functools.partial(kernel, sections, dp_size, tok, feat),
        out_shape=(
            jax.ShapeDtypeStruct((CHUNKS, tok, cw), BF16),
            jax.ShapeDtypeStruct((CHUNKS, tok, cw), BF16),
            jax.ShapeDtypeStruct((8, 128), F32),
            jax.ShapeDtypeStruct((4, piece, cw), BF16),
        ),
        in_specs=[anywhere, anywhere, anywhere, vmem, vmem, vmem, anywhere],
        out_specs=(anywhere, anywhere, anywhere, anywhere),
        scratch_shapes=[
            pltpu.VMEM((feat, feat), BF16),
            pltpu.VMEM((feat, feat), BF16),
            pltpu.VMEM((micros, CHUNKS, pair, cw), BF16),
            pltpu.VMEM((micros, CHUNKS, pair, cw), BF16),
            pltpu.VMEM((micros, CHUNKS, pair, cw), BF16),
            pltpu.VMEM((pair, feat), BF16),
            pltpu.VMEM((micros, halves, pair, ncols), BF16),
            pltpu.VMEM((micros, CHUNKS, pair, cw), BF16),
            pltpu.VMEM((micros, chips, pair, ncols), BF16),
            pltpu.VMEM((micros, chips, pair, cw), BF16),
            pltpu.VMEM((micros, CHUNKS, tok, cw), F32),
            pltpu.VMEM((micros, CHUNKS, tok, cw), F32),
            pltpu.VMEM((CHUNKS, pair, cw), F32),
            pltpu.VMEM((micros, 4, tok, 128), F32),
            pltpu.VMEM((micros, 8, 128), F32),
            pltpu.VMEM((micros, 8, 128), F32),
            pltpu.VMEM((keep, cw), BF16),
            dma((CHUNKS,)),
            dma((micros,)),
            dma((micros, CHUNKS)),
            dma((micros, CHUNKS)),
            dma((micros, CHUNKS)),
            dma((micros, CHUNKS)),
            dma((micros,)),
            dma((micros,)),
            dma((micros,)),
            dma((micros,)),
            dma((CHUNKS,)),
            dma((CHUNKS,)),
            dma((micros,)),
            dma,
            dma,
            dma,
            dma((keep // 256,)),
            dma((keep // 256,)),
            dma((4,)),
            dma((4,)),
        ],
        compiler_params=pltpu.CompilerParams(
            collective_id=0, has_side_effects=True, vmem_limit_bytes=63 * 2**20
        ),
    )(*operands)


def body(
    state,
    adjoint,
    probe,
    logp,
    density_weight,
    step_size,
    norm_gain,
    norm_shift,
    branch_gate,
    weights,
):
    sections = lax.axis_size("section")
    dp_size = lax.axis_size("dp")
    section_index = lax.axis_index("section")
    micros, tok, feat = state.shape
    cw = feat // CHUNKS

    def chunked(top, low):
        both = jnp.stack([top, low.astype(BF16)], axis=1)
        shaped = both.reshape(micros, 2 * tok, CHUNKS, cw)
        return shaped.transpose(0, 2, 1, 3)

    scale = jnp.broadcast_to(-density_weight[:, :, None], (micros, 8, 128))
    top, back, div, grad = run_kernel(
        sections,
        dp_size,
        tok,
        feat,
        chunked(state, probe),
        chunked(adjoint, probe),
        scale,
        norm_gain,
        norm_shift,
        branch_gate,
        weights[0],
    )

    def own(stack):
        return lax.dynamic_index_in_dim(stack, section_index, 0, keepdims=False)

    def rows(chunks):
        return chunks.transpose(1, 0, 2).reshape(tok, feat).astype(F32)

    step_value = step_size[0]
    own_input = own(state).astype(F32)
    state_next = own_input - step_value * (rows(top) - own_input)
    own_adjoint = own(adjoint).astype(F32)
    adjoint_next = own_adjoint + step_value * (rows(back) - own_adjoint)
    divergence = jnp.sum(div) / (tok * feat)
    logp_next = own(logp)[None] + step_value * divergence
    grad_rows = grad.transpose(1, 0, 2).reshape(feat // dp_size, feat).astype(F32)
    return (state_next[None], adjoint_next[None], logp_next, grad_rows[None])


def solution(mesh):
    placed = (
        P(None, "dp", None),
        P(None, "dp", None),
        P(None, "dp", None),
        P(None, "dp"),
        P(None, "dp"),
        P(),
        P("section", None),
        P("section", None),
        P("section", None),
        P("section", None, None),
    )
    return jax.shard_map(
        body,
        mesh=mesh,
        in_specs=placed,
        out_specs=(
            P("section", "dp", None),
            P("section", "dp", None),
            P("section", "dp"),
            P("section", "dp", None),
        ),
        check_vma=False,
    )
```

```python
import functools

import jax
import jax.numpy as jnp
from jax import lax
from jax.experimental import pallas as pl
from jax.experimental.pallas import tpu as pltpu
from jax.sharding import PartitionSpec as P

EPSILON = 1e-06
MESH = pl.DeviceIdType.MESH
CHUNKS = 4
LHS_ROWS = 128
ROOT_HALF = 0.7071067811865476
PHI_SCALE = 0.3989422804014327
F32 = jnp.float32
BF16 = jnp.bfloat16


def wait_bytes(ref, sem):
    pltpu.make_async_copy(ref, ref, sem).wait()


def lanes(value):
    total = value[:, 0:128]
    for at in range(128, value.shape[1], 128):
        total = total + value[:, at : at + 128]
    return total


def row_mean(value, inv):
    return jnp.sum(value, axis=1, keepdims=True) * inv


def kernel(
    sections, dp_size, tok, feat,
    state_hbm, adjoint_hbm, probe_hbm, logp_ref, dw_ref, step_ref, gain_ref, shift_ref, gate_ref, w_hbm,
    state_out, adjoint_out, logp_out, grad_out, n_hbm,
    w_vm, wt_vm, x_in, out_buf, c_in, n_buf, n_loc, g_all,
    g1_buf, g2_buf, c_buf, stats, rs_in, rs_out, signs, own_sign, own_state, own_adjoint, ex_recv, grad_acc,
    w_sem, in_sem, sign_sem, own_sem, x_ssem, x_rsem, c_ssem, c_rsem, rs_ssem, rs_rsem,
    n_ssem, n_rsem, g_ssem, g_rsem, load_sem, e_ssem, e_rsem, f_ssem, f_rsem,
):
    micros = sections
    cw = feat // CHUNKS
    pair = 2 * tok
    chips = dp_size // 2
    halves = chips // 4
    ncols = feat // halves
    keep = ncols // 2
    piece = keep // 4
    tile = keep // 2
    block_side = 256
    inv = 1.0 / feat
    half_section = sections // 2
    last = sections - 1
    spare = micros

    s = lax.axis_index("section")
    d = lax.axis_index("dp")
    core = lax.rem(d, 2)
    chip = lax.div(d, 2)
    x_at = lax.rem(chip, 2)
    d_flip = d + 2 - 4 * x_at
    my_half = lax.div(chip, 4)
    my_col = lax.rem(chip, 4)
    next_d = jnp.where(s == half_section - 1, d_flip, d)
    prev_d = jnp.where(s == half_section, d_flip, d)

    def chunk(k):
        return pl.ds(k * cw, cw)

    top = pl.ds(0, tok)
    low = pl.ds(tok, tok)
    both = pl.ds(0, pair)
    early = 256 if cw == 768 else 128
    parts = [(0, 0, early), (0, early, cw - early)] + [(k, 0, cw) for k in range(1, CHUNKS)]

    def w_copy(k):
        return pltpu.make_async_copy(w_hbm.at[:, chunk(k)], w_vm.at[:, chunk(k)], w_sem.at[k])

    def sign_copy(m):
        return pltpu.make_async_copy(probe_hbm.at[m], signs.at[m], sign_sem.at[m])

    def state_copy(m, k):
        return pltpu.make_async_copy(
            state_hbm.at[m, :, chunk(k)], x_in.at[m, k, top], in_sem.at[m, k]
        )

    own_copies = (
        pltpu.make_async_copy(state_hbm.at[s], own_state, own_sem.at[0]),
        pltpu.make_async_copy(adjoint_hbm.at[s], own_adjoint, own_sem.at[1]),
        pltpu.make_async_copy(probe_hbm.at[s], own_sign, own_sem.at[2]),
    )
    edge = (s == 0) | (s == last)

    @pl.when(edge)
    def _():
        for m in range(micros):
            sign_copy(m).start()

    @pl.when(s == 0)
    def _():
        for m in range(micros):
            for k in range(CHUNKS):
                state_copy(m, k).start()

    for k in range(CHUNKS):
        w_copy(k).start()
    for copy in own_copies:
        copy.start()
    n_buf[...] = jnp.zeros_like(n_buf)

    barrier = pltpu.get_barrier_semaphore()

    def greet_group(i, carry):
        other = lax.rem(d + i, dp_size)
        pl.semaphore_signal(barrier, inc=1, device_id=(s, other), device_id_type=MESH)
        return carry

    def greet_sections(i, carry):
        other = lax.rem(s + i, sections)
        pl.semaphore_signal(barrier, inc=1, device_id=(other, d), device_id_type=MESH)
        pl.semaphore_signal(barrier, inc=1, device_id=(other, d_flip), device_id_type=MESH)
        return carry

    lax.fori_loop(1, dp_size, greet_group, 0)
    lax.fori_loop(1, sections, greet_sections, 0)

    @pl.when(s == 0)
    def _():
        for m in range(micros):
            sign_copy(m).wait()
            for k in range(CHUNKS):
                x_in[m, k, low, :] = signs[m, :, chunk(k)].astype(BF16)

    @pl.when(s == last)
    def _():
        for m in range(micros):
            sign_copy(m).wait()
            for k in range(CHUNKS):
                out_buf[m, k, low, :] = signs[m, :, chunk(k)].astype(BF16)

    pl.semaphore_wait(barrier, dp_size - 1 + 2 * (sections - 1))

    lane = lax.broadcasted_iota(jnp.int32, (tok, 128), 1)

    def seed_copy(src, m, k, where):
        return pltpu.make_async_remote_copy(
            src_ref=src,
            dst_ref=c_in.at[m, k, where],
            send_sem=c_ssem.at[m, k],
            recv_sem=c_rsem.at[m, k],
            device_id=(s, d_flip),
            device_id_type=MESH,
        )

    def scalar_seed(m):
        return pltpu.make_async_remote_copy(
            src_ref=rs_out.at[m],
            dst_ref=rs_in.at[m],
            send_sem=rs_ssem.at[m],
            recv_sem=rs_rsem.at[m],
            device_id=(s, d_flip),
            device_id_type=MESH,
        )

    @pl.when(s == last)
    def _():
        for m in range(micros):
            weight = jnp.broadcast_to(dw_ref[m : m + 1, 0:1], (tok, 128))
            rs_out[m] = jnp.where(lane == 5, -weight, 0.0)
            scalar_seed(m).start()
            for k in range(CHUNKS):
                seed_copy(adjoint_hbm.at[m, :, chunk(k)], m, k, top).start()
                seed_copy(out_buf.at[m, k, low], m, k, low).start()

    def transpose_weights():
        count = feat // block_side

        def one(i, carry):
            at_row = pl.multiple_of(lax.div(i, count) * block_side, block_side)
            at_col = pl.multiple_of(lax.rem(i, count) * block_side, block_side)
            wt_vm[pl.ds(at_col, block_side), pl.ds(at_row, block_side)] = w_vm[
                pl.ds(at_row, block_side), pl.ds(at_col, block_side)
            ].T
            return carry

        lax.fori_loop(0, count * count, one, 0)

    @pl.when(s >= half_section)
    def _():
        for k in range(CHUNKS):
            w_copy(k).wait()
        transpose_weights()

    @pl.when(s == last)
    def _():
        for m in range(micros):
            scalar_seed(m).wait_send()
            for k in range(CHUNKS):
                wait_bytes(out_buf.at[m, k], c_ssem.at[m, k])

    def x_send(m, k, at, width):
        cols = pl.ds(at, width)
        return pltpu.make_async_remote_copy(
            src_ref=out_buf.at[m, k, both, cols],
            dst_ref=x_in.at[m, k, both, cols],
            send_sem=x_ssem.at[m, k],
            recv_sem=x_rsem.at[m, k],
            device_id=(s + 1, next_d),
            device_id_type=MESH,
        )

    def top_send(m, k, at, width):
        cols = pl.ds(at, width)
        return pltpu.make_async_remote_copy(
            src_ref=out_buf.at[m, k, top, cols],
            dst_ref=x_in.at[spare, k, top, cols],
            send_sem=x_ssem.at[m, k],
            recv_sem=x_rsem.at[spare, k],
            device_id=(m, d_flip),
            device_id_type=MESH,
        )

    def n_send(m, i):
        other = lax.rem(chip + i, chips)
        return pltpu.make_async_remote_copy(
            src_ref=n_loc.at[m, lax.div(other, 4)],
            dst_ref=n_hbm.at[m, pl.ds(chip * pair, pair)],
            send_sem=n_ssem.at[m],
            recv_sem=n_rsem.at[m],
            device_id=(s, other * 2 + core),
            device_id_type=MESH,
        )

    def n_own(m):
        return pltpu.make_async_copy(
            n_loc.at[m, my_half], n_hbm.at[m, pl.ds(chip * pair, pair)], load_sem.at[m]
        )

    def forward(m, carry):
        def rows(k):
            return x_in[m, k, top, :].astype(F32)

        def tangents(k):
            return x_in[m, k, low, :].astype(F32)

        total_u = total_w = square = cross = 0.0
        for k in range(CHUNKS):

            @pl.when(s > 0)
            def _():
                wait_bytes(x_in.at[m, k], x_rsem.at[m, k])

            u = rows(k)
            w = tangents(k)
            if k == 0:
                base_u = row_mean(lanes(u), 1.0 / cw)
                base_w = row_mean(lanes(w), 1.0 / cw)
            u = u - base_u
            w = w - base_w
            total_u = total_u + lanes(u)
            total_w = total_w + lanes(w)
            square = square + lanes(u * u)
            cross = cross + lanes(u * w)
        shift_u = row_mean(total_u, inv)
        shift_w = row_mean(total_w, inv)
        var = row_mean(square, inv) - shift_u * shift_u
        cov = row_mean(cross, inv) - shift_u * shift_w
        mean_u = base_u + shift_u
        mean_w = base_w + shift_w
        rinv = lax.rsqrt(jnp.maximum(var, 0.0) + EPSILON)
        slope = rinv * cov
        for at, value in enumerate((mean_u, mean_w, rinv, slope)):
            stats[m, at] = jnp.broadcast_to(value, (tok, 128))
        for k in range(CHUNKS):
            gain = gain_ref[:, chunk(k)]
            xhat = (rows(k) - mean_u) * rinv
            normed = xhat * gain + shift_ref[:, chunk(k)]
            normed_t = rinv * ((tangents(k) - mean_w) - xhat * slope) * gain
            n_buf[top, chunk(k)] = normed.astype(BF16)
            n_buf[low, chunk(k)] = normed_t.astype(BF16)

        for k, at, width in parts:
            cols = pl.ds(at, width)
            wide = pl.ds(k * cw + at, width)
            if at == 0:

                @pl.when((m == 0) & (s < half_section))
                def _():
                    w_copy(k).wait()

            product = jnp.dot(n_buf[...], w_vm[:, wide], preferred_element_type=F32)
            z = product[:tok]
            z_t = product[tok:pair]
            gate = gate_ref[:, wide]
            cdf = 0.5 + 0.5 * lax.erf(z * ROOT_HALF)
            zz = z * z
            pdf = PHI_SCALE * jnp.exp(-0.5 * zz)
            first = gate * (cdf + z * pdf)
            u = x_in[m, k, top, cols].astype(F32)
            w = x_in[m, k, low, cols].astype(F32)
            out_buf[m, k, top, cols] = (u + gate * (z * cdf)).astype(BF16)
            out_buf[m, k, low, cols] = (w + first * z_t).astype(BF16)

            @pl.when(s < last)
            def _():
                x_send(m, k, at, width).start()

            @pl.when(s == last)
            def _():
                top_send(m, k, at, width).start()

            g1_buf[m, k, :, cols] = first
            g2_buf[m, k, :, cols] = gate * (pdf * (2.0 - zz)) * z_t
            if k == 0 and at == 0:
                for half in range(halves):
                    n_loc[m, half] = n_buf[both, pl.ds(half * ncols, ncols)]
                for i in range(1, chips):
                    n_send(m, i).start()
                n_own(m).start()
        return carry

    @pl.when(s == 0)
    def _():
        for m in range(micros):
            for k in range(CHUNKS):
                state_copy(m, k).wait()

    lax.fori_loop(0, micros, forward, 0)

    @pl.when(s < half_section)
    def _():
        transpose_weights()

    pitch = micros * pair

    def c_out(m, k):
        return w_vm.at[pl.ds(pl.multiple_of(m * pair, pair), pair), chunk(k)]

    def g_loc(m, k):
        return w_vm.at[pl.ds(pl.multiple_of(pitch + m * pair, pair), pair), chunk(k)]

    def c_send(m, k, at, width):
        return pltpu.make_async_remote_copy(
            src_ref=c_out(m, k).at[both, pl.ds(at, width)],
            dst_ref=c_in.at[m, k, both, pl.ds(at, width)],
            send_sem=c_ssem.at[m, k],
            recv_sem=c_rsem.at[m, k],
            device_id=(s - 1, prev_d),
            device_id_type=MESH,
        )

    def back_send(m, k, at, width):
        return pltpu.make_async_remote_copy(
            src_ref=c_out(m, k).at[top, pl.ds(at, width)],
            dst_ref=c_in.at[spare, k, top, pl.ds(at, width)],
            send_sem=c_ssem.at[m, k],
            recv_sem=c_rsem.at[spare, k],
            device_id=(m, jnp.where(m == 0, d_flip, d)),
            device_id_type=MESH,
        )

    def scalar_send(m):
        slot = jnp.where(s == 0, spare, m)
        return pltpu.make_async_remote_copy(
            src_ref=rs_out.at[m],
            dst_ref=rs_in.at[slot],
            send_sem=rs_ssem.at[m],
            recv_sem=rs_rsem.at[slot],
            device_id=(
                jnp.where(s == 0, m, s - 1),
                jnp.where((s == 0) & (m == 0), d_flip, prev_d),
            ),
            device_id_type=MESH,
        )

    def g_send(m, i):
        other = lax.rem(chip + i, chips)
        cols = pl.ds(pl.multiple_of(lax.rem(other, 4) * cw, cw), cw)
        return pltpu.make_async_remote_copy(
            src_ref=w_vm.at[pl.ds(pl.multiple_of(pitch + m * pair, pair), pair), cols],
            dst_ref=g_all.at[m, chip],
            send_sem=g_ssem.at[m],
            recv_sem=g_rsem.at[m],
            device_id=(s, other * 2 + core),
            device_id_type=MESH,
        )

    def backward(m, carry):
        for k in range(CHUNKS):
            wait_bytes(c_in.at[m, k], c_rsem.at[m, k])
        wait_bytes(rs_in.at[m], rs_rsem.at[m])
        scalars = rs_in[m]
        add_u, by_u, by_w, add_t, by_t, factor, told = (scalars[:, i : i + 1] for i in range(7))
        moved = 0.0
        for k in range(CHUNKS):
            u = out_buf[m, k, top, :].astype(F32)
            w = out_buf[m, k, low, :].astype(F32)
            c = c_in[m, k, top, :].astype(F32) + (add_u + by_u * u + by_w * w)
            sign = c_in[m, k, low, :].astype(F32)
            moved = moved + lanes(sign * (w - sign))
            c_t = sign * factor + (add_t + by_t * u)
            c_buf[k, top, :] = c
            c_buf[k, low, :] = c_t
            first = g1_buf[m, k]
            n_buf[top, chunk(k)] = (c * first + c_t * g2_buf[m, k]).astype(BF16)
            n_buf[low, chunk(k)] = (c_t * first).astype(BF16)

        mean_u = stats[m, 0][:, 0:1]
        mean_w = stats[m, 1][:, 0:1]
        rinv = stats[m, 2][:, 0:1]
        slope = stats[m, 3][:, 0:1]
        square = rinv * rinv
        lean = square * slope

        sums = [0.0] * 5
        for k, at, width in parts:
            cols = pl.ds(at, width)
            wide = pl.ds(k * cw + at, width)
            product = jnp.dot(n_buf[...], wt_vm[:, wide], preferred_element_type=F32)
            gain = gain_ref[:, wide]
            a = product[:tok] * gain
            b = product[tok:pair] * gain
            out = c_out(m, k)
            out[top, cols] = (c_buf[k, top, cols] + rinv * a - lean * b).astype(BF16)
            out[low, cols] = (c_buf[k, low, cols] + rinv * b).astype(BF16)

            @pl.when(s > 0)
            def _():
                c_send(m, k, at, width).start()

            @pl.when(s == 0)
            def _():
                back_send(m, k, at, width).start()

            xhat = (x_in[m, k, top, cols].astype(F32) - mean_u) * rinv
            centered = x_in[m, k, low, cols].astype(F32) - mean_w
            for i, value in enumerate((a, a * xhat, b, b * xhat, b * centered)):
                sums[i] = sums[i] + lanes(value)
            if k == 0 and at == 0:
                for j in range(CHUNKS):
                    g_loc(m, j)[...] = n_buf[both, chunk(j)]
                for i in range(1, chips):
                    g_send(m, i).start()
        mean_a, mean_ax, mean_b, mean_bx, mean_bw = (row_mean(value, inv) for value in sums)
        beta = -rinv * mean_ax - square * (mean_bw - 3.0 * mean_bx * slope)
        gamma = -square * mean_bx
        alpha = lean * mean_b - rinv * mean_a
        values = (
            alpha - beta * rinv * mean_u - gamma * mean_w,
            beta * rinv,
            gamma,
            -rinv * mean_b - gamma * mean_u,
            gamma,
            1.0,
            jnp.where(s == last, jnp.sum(moved, axis=1, keepdims=True), told),
        )
        packed = 0.0
        for at, value in enumerate(values):
            packed = jnp.where(lane == at, value, packed)
        rs_out[m] = packed
        scalar_send(m).start()
        g_all[m, chip] = own_block(m)
        return carry

    def own_block(m):
        cols = pl.ds(pl.multiple_of(my_col * cw, cw), cw)
        return w_vm[pl.ds(pl.multiple_of(pitch + m * pair, pair), pair), cols]

    lax.fori_loop(0, micros, backward, 0)

    base = 2 * pitch
    depth = chips * pair

    def n_load(m):
        return pltpu.make_async_copy(
            n_hbm.at[m], w_vm.at[pl.ds(base + m * depth, depth), pl.ds(0, ncols)], load_sem.at[m]
        )

    for m in range(micros):
        n_own(m).wait()
        wait_bytes(n_hbm.at[m, pl.ds(0, depth - pair)], n_rsem.at[m])
        n_load(m).start()
    spot = base if halves > 1 else base + micros * depth
    ex_send = w_vm.at[pl.ds(spot, keep), pl.ds(feat // 2, cw)]
    fin_send = w_vm.at[pl.ds(spot, keep), pl.ds(feat // 2 + cw, cw)]
    most = micros * 3 // 4

    def block(start, first, count):
        cols = pl.ds(pl.multiple_of(start, 128), tile)
        left = w_vm[pl.ds(base + first * depth, count * depth), cols]
        right = g_all[pl.ds(first, count)].reshape(count * depth, cw)
        return lax.dot_general(left, right, (((0,), (0,)), ((), ())), preferred_element_type=F32)

    def gathered(first, count):
        for m in range(first, first + count):
            wait_bytes(g_all.at[m, pl.ds(0, chips - 1)], g_rsem.at[m])
            n_load(m).wait()

    starts = [(1 - core) * keep, (1 - core) * keep + tile, core * keep, core * keep + tile]
    gathered(0, most)
    for i in range(4):
        grad_acc[i] = block(starts[i], 0, most)
    gathered(most, micros - most)

    def ex_copy(i):
        at = pl.ds(i * tile, tile)
        return pltpu.make_async_remote_copy(
            src_ref=ex_send.at[at],
            dst_ref=ex_recv.at[at],
            send_sem=e_ssem.at[i],
            recv_sem=e_rsem.at[i],
            device_id=(s, d + 1 - 2 * core),
            device_id_type=MESH,
        )

    goal = (2 * my_half + core) * 4
    grad_cols = pl.ds(pl.multiple_of(my_col * cw, cw), cw)

    def piece_send(j):
        return pltpu.make_async_remote_copy(
            src_ref=fin_send.at[pl.ds(j * piece, piece)],
            dst_ref=grad_out.at[:, grad_cols],
            send_sem=f_ssem.at[j],
            recv_sem=f_rsem.at[my_col],
            device_id=(s, goal + j),
            device_id_type=MESH,
        )

    def piece_own(j):
        return pltpu.make_async_copy(
            fin_send.at[pl.ds(j * piece, piece)], grad_out.at[:, grad_cols], f_rsem.at[my_col]
        )

    for i in range(2):
        ex_send[pl.ds(i * tile, tile), :] = (
            grad_acc[i] + block(starts[i], most, micros - most)
        ).astype(BF16)
        ex_copy(i).start()
    for i in range(2):
        at = pl.ds(i * tile, tile)
        mine = grad_acc[2 + i] + block(starts[2 + i], most, micros - most)
        wait_bytes(ex_recv.at[at], e_rsem.at[i])
        fin_send[at, :] = (mine + ex_recv[at, :].astype(F32)).astype(BF16)
        for j in (2 * i, 2 * i + 1):

            @pl.when(goal + j != d)
            def _():
                piece_send(j).start()

            @pl.when(goal + j == d)
            def _():
                piece_own(j).start()

    for copy in own_copies:
        copy.wait()
    for k in range(CHUNKS):
        wait_bytes(x_in.at[spare, k, top], x_rsem.at[spare, k])
        wait_bytes(c_in.at[spare, k, top], c_rsem.at[spare, k])
    wait_bytes(rs_in.at[spare], rs_rsem.at[spare])
    step = step_ref[...]
    scalars = jnp.where(s == 0, rs_out[0], rs_in[spare])
    for k in range(CHUNKS):
        sign = own_sign[:, chunk(k)].astype(F32)
        start = own_state[:, chunk(k)].astype(F32)
        first = own_adjoint[:, chunk(k)].astype(F32)
        final_u = x_in[spare, k, top, :].astype(F32)
        state_out[:, chunk(k)] = start - step * (final_u - start)
        back = jnp.where(s == 0, c_out(0, k)[top, :].astype(F32), c_in[spare, k, top, :].astype(F32))
        back = back + (scalars[:, 0:1] + scalars[:, 1:2] * start + scalars[:, 2:3] * sign)
        adjoint_out[:, chunk(k)] = first + step * (back - first)
    summed = jnp.sum(scalars[:, 6:7], axis=0, keepdims=True)
    which = lax.broadcasted_iota(jnp.int32, (micros, 1), 0)
    mine = jnp.sum(jnp.where(which == s, logp_ref[...], 0.0), axis=0, keepdims=True)
    logp_out[...] = mine + step * (summed / (tok * feat))

    def drain(m, carry):
        wait_bytes(n_hbm.at[m, pl.ds(0, depth - pair)], n_ssem.at[m])
        wait_bytes(g_all.at[m, pl.ds(0, chips - 1)], g_ssem.at[m])
        scalar_send(m).wait_send()

        @pl.when(s < last)
        def _():
            for k in range(CHUNKS):
                wait_bytes(out_buf.at[m, k], x_ssem.at[m, k])

        @pl.when(s == last)
        def _():
            for k in range(CHUNKS):
                wait_bytes(out_buf.at[m, k, top], x_ssem.at[m, k])

        @pl.when(s > 0)
        def _():
            for k in range(CHUNKS):
                wait_bytes(c_in.at[m, k], c_ssem.at[m, k])

        @pl.when(s == 0)
        def _():
            for k in range(CHUNKS):
                wait_bytes(c_in.at[m, k, top], c_ssem.at[m, k])

        return carry

    lax.fori_loop(0, micros, drain, 0)
    for i in range(2):
        ex_copy(i).wait_send()
    for j in range(4):

        @pl.when(goal + j != d)
        def _():
            piece_send(j).wait_send()

        wait_bytes(grad_out.at[:, chunk(j)], f_rsem.at[j])


def run_kernel(sections, dp_size, tok, feat, *operands):
    micros = sections
    cw = feat // CHUNKS
    pair = 2 * tok
    chips = dp_size // 2
    halves = chips // 4
    ncols = feat // halves
    keep = ncols // 2
    piece = keep // 4
    dma = pltpu.SemaphoreType.DMA
    anywhere = pl.BlockSpec(memory_space=pl.ANY)
    vmem = pl.BlockSpec(memory_space=pltpu.VMEM)
    return pl.pallas_call(
        functools.partial(kernel, sections, dp_size, tok, feat),
        out_shape=(
            jax.ShapeDtypeStruct((tok, feat), F32),
            jax.ShapeDtypeStruct((tok, feat), F32),
            jax.ShapeDtypeStruct((1, 1), F32),
            jax.ShapeDtypeStruct((piece, feat), BF16),
            jax.ShapeDtypeStruct((micros, chips * pair, ncols), BF16),
        ),
        in_specs=[anywhere] * 3 + [vmem] * 6 + [anywhere],
        out_specs=(vmem, vmem, vmem, anywhere, anywhere),
        scratch_shapes=[
            pltpu.VMEM((feat, feat), BF16),
            pltpu.VMEM((feat, feat), BF16),
            pltpu.VMEM((micros + 1, CHUNKS, pair, cw), BF16),
            pltpu.VMEM((micros, CHUNKS, pair, cw), BF16),
            pltpu.VMEM((micros + 1, CHUNKS, pair, cw), BF16),
            pltpu.VMEM((LHS_ROWS, feat), BF16),
            pltpu.VMEM((micros, halves, pair, ncols), BF16),
            pltpu.VMEM((micros, chips, pair, cw), BF16),
            pltpu.VMEM((micros, CHUNKS, tok, cw), F32),
            pltpu.VMEM((micros, CHUNKS, tok, cw), F32),
            pltpu.VMEM((CHUNKS, pair, cw), F32),
            pltpu.VMEM((micros, 4, tok, 128), F32),
            pltpu.VMEM((micros + 1, tok, 128), F32),
            pltpu.VMEM((micros, tok, 128), F32),
            pltpu.VMEM((micros, tok, feat), jnp.int32),
            pltpu.VMEM((tok, feat), jnp.int32),
            pltpu.VMEM((tok, feat), BF16),
            pltpu.VMEM((tok, feat), BF16),
            pltpu.VMEM((keep, cw), BF16),
            pltpu.VMEM((4, keep // 2, cw), F32),
            dma((CHUNKS,)),
            dma((micros, CHUNKS)),
            dma((micros,)),
            dma((3,)),
            dma((micros, CHUNKS)),
            dma((micros + 1, CHUNKS)),
            dma((micros, CHUNKS)),
            dma((micros + 1, CHUNKS)),
            dma((micros,)),
            dma((micros + 1,)),
            dma((micros,)),
            dma((micros,)),
            dma((micros,)),
            dma((micros,)),
            dma((micros,)),
            dma((2,)),
            dma((2,)),
            dma((4,)),
            dma((4,)),
        ],
        compiler_params=pltpu.CompilerParams(
            collective_id=0, has_side_effects=True, vmem_limit_bytes=63 * 2**20
        ),
    )(*operands)


def body(
    state,
    adjoint,
    probe,
    logp,
    density_weight,
    step_size,
    norm_gain,
    norm_shift,
    branch_gate,
    weights,
):
    _, tok, feat = state.shape
    state_next, adjoint_next, logp_next, grad, _ = run_kernel(
        lax.axis_size("section"),
        lax.axis_size("dp"),
        tok,
        feat,
        state,
        adjoint,
        probe,
        logp,
        density_weight,
        step_size[None],
        norm_gain,
        norm_shift,
        branch_gate,
        weights[0],
    )
    return (state_next[None], adjoint_next[None], logp_next, grad[None].astype(F32))


def solution(mesh):
    placed = (
        P(None, "dp", None),
        P(None, "dp", None),
        P(None, "dp", None),
        P(None, "dp"),
        P(None, "dp"),
        P(),
        P("section", None),
        P("section", None),
        P("section", None),
        P("section", None, None),
    )
    return jax.shard_map(
        body,
        mesh=mesh,
        in_specs=placed,
        out_specs=(
            P("section", "dp", None),
            P("section", "dp", None),
            P("section", "dp"),
            P("section", "dp", None),
        ),
        check_vma=False,
    )
```

```python
import functools

import jax
import jax.numpy as jnp
from jax import lax
from jax.experimental import pallas as pl
from jax.experimental.pallas import tpu as pltpu
from jax.sharding import PartitionSpec as P

EPSILON = 1e-06
MESH = pl.DeviceIdType.MESH
CHUNKS = 4
LHS_ROWS = 128
ROOT_HALF = 0.7071067811865476
PHI_SCALE = 0.3989422804014327
F32 = jnp.float32
BF16 = jnp.bfloat16


def wait_bytes(ref, sem):
    pltpu.make_async_copy(ref, ref, sem).wait()


def lanes(value):
    total = value[:, 0:128]
    for at in range(128, value.shape[1], 128):
        total = total + value[:, at : at + 128]
    return total


def row_mean(value, inv):
    return jnp.sum(value, axis=1, keepdims=True) * inv


def kernel(
    sections, dp_size, tok, feat,
    state_hbm, adjoint_hbm, probe_hbm, logp_ref, dw_ref, step_ref, gain_ref, shift_ref, gate_ref, w_hbm,
    state_out, adjoint_out, logp_out, grad_out, n_hbm,
    w_vm, wt_vm, x_in, out_buf, c_in, n_buf, n_loc, g_all,
    g1_buf, g2_buf, c_buf, stats, rs_in, rs_out, signs, own_sign, own_state, own_adjoint, ex_recv, grad_acc,
    w_sem, in_sem, sign_sem, own_sem, x_ssem, x_rsem, c_ssem, c_rsem, rs_ssem, rs_rsem,
    n_ssem, n_rsem, g_ssem, g_rsem, load_sem, e_ssem, e_rsem, f_ssem, f_rsem,
):
    micros = sections
    cw = feat // CHUNKS
    pair = 2 * tok
    chips = dp_size // 2
    halves = chips // 4
    ncols = feat // halves
    keep = ncols // 2
    piece = keep // 4
    tile = keep // 2
    block_side = 256
    inv = 1.0 / feat
    half_section = sections // 2
    last = sections - 1
    spare = micros

    s = lax.axis_index("section")
    d = lax.axis_index("dp")
    core = lax.rem(d, 2)
    chip = lax.div(d, 2)
    x_at = lax.rem(chip, 2)
    d_flip = d + 2 - 4 * x_at + 1 - 2 * core
    my_half = lax.div(chip, 4)
    my_col = lax.rem(chip, 4)
    next_d = jnp.where(s == half_section - 1, d_flip, d)
    prev_d = jnp.where(s == half_section, d_flip, d)

    def chunk(k):
        return pl.ds(k * cw, cw)

    top = pl.ds(0, tok)
    low = pl.ds(tok, tok)
    both = pl.ds(0, pair)
    early = 256 if cw == 768 else 128
    parts = [(0, 0, early), (0, early, cw - early)] + [(k, 0, cw) for k in range(1, CHUNKS)]

    def w_copy(k):
        return pltpu.make_async_copy(w_hbm.at[:, chunk(k)], w_vm.at[:, chunk(k)], w_sem.at[k])

    def sign_copy(m):
        return pltpu.make_async_copy(probe_hbm.at[m], signs.at[m], sign_sem.at[m])

    def state_copy(m, k):
        return pltpu.make_async_copy(
            state_hbm.at[m, :, chunk(k)], x_in.at[m, k, top], in_sem.at[m, k]
        )

    own_copies = (
        pltpu.make_async_copy(state_hbm.at[s], own_state, own_sem.at[0]),
        pltpu.make_async_copy(adjoint_hbm.at[s], own_adjoint, own_sem.at[1]),
        pltpu.make_async_copy(probe_hbm.at[s], own_sign, own_sem.at[2]),
    )
    edge = (s == 0) | (s == last)

    @pl.when(edge)
    def _():
        for m in range(micros):
            sign_copy(m).start()

    @pl.when(s == 0)
    def _():
        for m in range(micros):
            for k in range(CHUNKS):
                state_copy(m, k).start()

    for k in range(CHUNKS):
        w_copy(k).start()
    for copy in own_copies:
        copy.start()
    n_buf[...] = jnp.zeros_like(n_buf)

    barrier = pltpu.get_barrier_semaphore()

    def greet_group(i, carry):
        other = lax.rem(d + i, dp_size)
        pl.semaphore_signal(barrier, inc=1, device_id=(s, other), device_id_type=MESH)
        return carry

    def greet_sections(i, carry):
        other = lax.rem(s + i, sections)
        pl.semaphore_signal(barrier, inc=1, device_id=(other, d), device_id_type=MESH)
        pl.semaphore_signal(barrier, inc=1, device_id=(other, d_flip), device_id_type=MESH)
        return carry

    lax.fori_loop(1, dp_size, greet_group, 0)
    lax.fori_loop(1, sections, greet_sections, 0)

    @pl.when(s == 0)
    def _():
        for m in range(micros):
            sign_copy(m).wait()
            for k in range(CHUNKS):
                x_in[m, k, low, :] = signs[m, :, chunk(k)].astype(BF16)

    @pl.when(s == last)
    def _():
        for m in range(micros):
            sign_copy(m).wait()
            for k in range(CHUNKS):
                out_buf[m, k, low, :] = signs[m, :, chunk(k)].astype(BF16)

    pl.semaphore_wait(barrier, dp_size - 1 + 2 * (sections - 1))

    lane = lax.broadcasted_iota(jnp.int32, (tok, 128), 1)

    def seed_copy(src, m, k, where):
        return pltpu.make_async_remote_copy(
            src_ref=src,
            dst_ref=c_in.at[m, k, where],
            send_sem=c_ssem.at[m, k],
            recv_sem=c_rsem.at[m, k],
            device_id=(s, d_flip),
            device_id_type=MESH,
        )

    def scalar_seed(m):
        return pltpu.make_async_remote_copy(
            src_ref=rs_out.at[m],
            dst_ref=rs_in.at[m],
            send_sem=rs_ssem.at[m],
            recv_sem=rs_rsem.at[m],
            device_id=(s, d_flip),
            device_id_type=MESH,
        )

    @pl.when(s == last)
    def _():
        for m in range(micros):
            weight = jnp.broadcast_to(dw_ref[0:1, m : m + 1], (tok, 128))
            rs_out[m] = jnp.where(lane == 5, -weight, 0.0)
            scalar_seed(m).start()
            for k in range(CHUNKS):
                seed_copy(adjoint_hbm.at[m, :, chunk(k)], m, k, top).start()
                seed_copy(out_buf.at[m, k, low], m, k, low).start()

    def transpose_weights():
        count = feat // block_side

        def one(i, carry):
            at_row = pl.multiple_of(lax.div(i, count) * block_side, block_side)
            at_col = pl.multiple_of(lax.rem(i, count) * block_side, block_side)
            wt_vm[pl.ds(at_col, block_side), pl.ds(at_row, block_side)] = w_vm[
                pl.ds(at_row, block_side), pl.ds(at_col, block_side)
            ].T
            return carry

        lax.fori_loop(0, count * count, one, 0)

    @pl.when(s >= half_section)
    def _():
        for k in range(CHUNKS):
            w_copy(k).wait()
        transpose_weights()

    @pl.when(s == last)
    def _():
        for m in range(micros):
            scalar_seed(m).wait_send()
            for k in range(CHUNKS):
                wait_bytes(out_buf.at[m, k], c_ssem.at[m, k])

    def x_send(m, k, at, width):
        cols = pl.ds(at, width)
        return pltpu.make_async_remote_copy(
            src_ref=out_buf.at[m, k, both, cols],
            dst_ref=x_in.at[m, k, both, cols],
            send_sem=x_ssem.at[m, k],
            recv_sem=x_rsem.at[m, k],
            device_id=(s + 1, next_d),
            device_id_type=MESH,
        )

    def top_send(m, k, at, width):
        cols = pl.ds(at, width)
        return pltpu.make_async_remote_copy(
            src_ref=out_buf.at[m, k, top, cols],
            dst_ref=x_in.at[spare, k, top, cols],
            send_sem=x_ssem.at[m, k],
            recv_sem=x_rsem.at[spare, k],
            device_id=(m, d_flip),
            device_id_type=MESH,
        )

    def n_send(m, i):
        other = lax.rem(chip + i, chips)
        return pltpu.make_async_remote_copy(
            src_ref=n_loc.at[m, lax.div(other, 4)],
            dst_ref=n_hbm.at[m, pl.ds(chip * pair, pair)],
            send_sem=n_ssem.at[m],
            recv_sem=n_rsem.at[m],
            device_id=(s, other * 2 + core),
            device_id_type=MESH,
        )

    def n_own(m):
        return pltpu.make_async_copy(
            n_loc.at[m, my_half], n_hbm.at[m, pl.ds(chip * pair, pair)], load_sem.at[m]
        )

    def forward(m, carry):
        def rows(k):
            return x_in[m, k, top, :].astype(F32)

        def tangents(k):
            return x_in[m, k, low, :].astype(F32)

        total_u = total_w = square = cross = 0.0
        for k in range(CHUNKS):

            @pl.when(s > 0)
            def _():
                wait_bytes(x_in.at[m, k], x_rsem.at[m, k])

            u = rows(k)
            w = tangents(k)
            if k == 0:
                base_u = row_mean(lanes(u), 1.0 / cw)
                base_w = row_mean(lanes(w), 1.0 / cw)
            u = u - base_u
            w = w - base_w
            total_u = total_u + lanes(u)
            total_w = total_w + lanes(w)
            square = square + lanes(u * u)
            cross = cross + lanes(u * w)
        shift_u = row_mean(total_u, inv)
        shift_w = row_mean(total_w, inv)
        var = row_mean(square, inv) - shift_u * shift_u
        cov = row_mean(cross, inv) - shift_u * shift_w
        mean_u = base_u + shift_u
        mean_w = base_w + shift_w
        rinv = lax.rsqrt(jnp.maximum(var, 0.0) + EPSILON)
        slope = rinv * cov
        for at, value in enumerate((mean_u, mean_w, rinv, slope)):
            stats[m, at] = jnp.broadcast_to(value, (tok, 128))
        for k in range(CHUNKS):
            gain = gain_ref[:, chunk(k)]
            xhat = (rows(k) - mean_u) * rinv
            normed = xhat * gain + shift_ref[:, chunk(k)]
            normed_t = rinv * ((tangents(k) - mean_w) - xhat * slope) * gain
            n_buf[top, chunk(k)] = normed.astype(BF16)
            n_buf[low, chunk(k)] = normed_t.astype(BF16)

        for k, at, width in parts:
            cols = pl.ds(at, width)
            wide = pl.ds(k * cw + at, width)
            if at == 0:

                @pl.when((m == 0) & (s < half_section))
                def _():
                    w_copy(k).wait()

            product = jnp.dot(n_buf[...], w_vm[:, wide], preferred_element_type=F32)
            z = product[:tok]
            z_t = product[tok:pair]
            gate = gate_ref[:, wide]
            cdf = 0.5 + 0.5 * lax.erf(z * ROOT_HALF)
            zz = z * z
            pdf = PHI_SCALE * jnp.exp(-0.5 * zz)
            first = gate * (cdf + z * pdf)
            u = x_in[m, k, top, cols].astype(F32)
            w = x_in[m, k, low, cols].astype(F32)
            out_buf[m, k, top, cols] = (u + gate * (z * cdf)).astype(BF16)
            out_buf[m, k, low, cols] = (w + first * z_t).astype(BF16)

            @pl.when(s < last)
            def _():
                x_send(m, k, at, width).start()

            @pl.when(s == last)
            def _():
                top_send(m, k, at, width).start()

            g1_buf[m, k, :, cols] = first
            g2_buf[m, k, :, cols] = gate * (pdf * (2.0 - zz)) * z_t
            if k == 0 and at == 0:
                for half in range(halves):
                    n_loc[m, half] = n_buf[both, pl.ds(half * ncols, ncols)]
                for i in range(1, chips):
                    n_send(m, i).start()
                n_own(m).start()
        return carry

    @pl.when(s == 0)
    def _():
        for m in range(micros):
            for k in range(CHUNKS):
                state_copy(m, k).wait()

    lax.fori_loop(0, micros, forward, 0)

    @pl.when(s < half_section)
    def _():
        transpose_weights()

    pitch = micros * pair

    def c_out(m, k):
        return w_vm.at[pl.ds(pl.multiple_of(m * pair, pair), pair), chunk(k)]

    def g_loc(m, k):
        return w_vm.at[pl.ds(pl.multiple_of(pitch + m * pair, pair), pair), chunk(k)]

    def c_send(m, k, at, width):
        return pltpu.make_async_remote_copy(
            src_ref=c_out(m, k).at[both, pl.ds(at, width)],
            dst_ref=c_in.at[m, k, both, pl.ds(at, width)],
            send_sem=c_ssem.at[m, k],
            recv_sem=c_rsem.at[m, k],
            device_id=(s - 1, prev_d),
            device_id_type=MESH,
        )

    def back_send(m, k, at, width):
        return pltpu.make_async_remote_copy(
            src_ref=c_out(m, k).at[top, pl.ds(at, width)],
            dst_ref=c_in.at[spare, k, top, pl.ds(at, width)],
            send_sem=c_ssem.at[m, k],
            recv_sem=c_rsem.at[spare, k],
            device_id=(m, jnp.where(m == 0, d_flip, d)),
            device_id_type=MESH,
        )

    def scalar_send(m):
        slot = jnp.where(s == 0, spare, m)
        return pltpu.make_async_remote_copy(
            src_ref=rs_out.at[m],
            dst_ref=rs_in.at[slot],
            send_sem=rs_ssem.at[m],
            recv_sem=rs_rsem.at[slot],
            device_id=(
                jnp.where(s == 0, m, s - 1),
                jnp.where((s == 0) & (m == 0), d_flip, prev_d),
            ),
            device_id_type=MESH,
        )

    def g_send(m, i):
        other = lax.rem(chip + i, chips)
        cols = pl.ds(pl.multiple_of(lax.rem(other, 4) * cw, cw), cw)
        return pltpu.make_async_remote_copy(
            src_ref=w_vm.at[pl.ds(pl.multiple_of(pitch + m * pair, pair), pair), cols],
            dst_ref=g_all.at[m, chip],
            send_sem=g_ssem.at[m],
            recv_sem=g_rsem.at[m],
            device_id=(s, other * 2 + core),
            device_id_type=MESH,
        )

    def backward(m, carry):
        for k in range(CHUNKS):
            wait_bytes(c_in.at[m, k], c_rsem.at[m, k])
        wait_bytes(rs_in.at[m], rs_rsem.at[m])
        scalars = rs_in[m]
        add_u, by_u, by_w, add_t, by_t, factor, told = (scalars[:, i : i + 1] for i in range(7))
        moved = 0.0
        for k in range(CHUNKS):
            u = out_buf[m, k, top, :].astype(F32)
            w = out_buf[m, k, low, :].astype(F32)
            c = c_in[m, k, top, :].astype(F32) + (add_u + by_u * u + by_w * w)
            sign = c_in[m, k, low, :].astype(F32)
            moved = moved + lanes(sign * (w - sign))
            c_t = sign * factor + (add_t + by_t * u)
            c_buf[k, top, :] = c
            c_buf[k, low, :] = c_t
            first = g1_buf[m, k]
            n_buf[top, chunk(k)] = (c * first + c_t * g2_buf[m, k]).astype(BF16)
            n_buf[low, chunk(k)] = (c_t * first).astype(BF16)

        mean_u = stats[m, 0][:, 0:1]
        mean_w = stats[m, 1][:, 0:1]
        rinv = stats[m, 2][:, 0:1]
        slope = stats[m, 3][:, 0:1]
        square = rinv * rinv
        lean = square * slope

        sums = [0.0] * 5
        for k, at, width in parts:
            cols = pl.ds(at, width)
            wide = pl.ds(k * cw + at, width)
            product = jnp.dot(n_buf[...], wt_vm[:, wide], preferred_element_type=F32)
            gain = gain_ref[:, wide]
            a = product[:tok] * gain
            b = product[tok:pair] * gain
            out = c_out(m, k)
            out[top, cols] = (c_buf[k, top, cols] + rinv * a - lean * b).astype(BF16)
            out[low, cols] = (c_buf[k, low, cols] + rinv * b).astype(BF16)

            @pl.when(s > 0)
            def _():
                c_send(m, k, at, width).start()

            @pl.when(s == 0)
            def _():
                back_send(m, k, at, width).start()

            xhat = (x_in[m, k, top, cols].astype(F32) - mean_u) * rinv
            centered = x_in[m, k, low, cols].astype(F32) - mean_w
            for i, value in enumerate((a, a * xhat, b, b * xhat, b * centered)):
                sums[i] = sums[i] + lanes(value)
            if k == 0 and at == 0:
                for j in range(CHUNKS):
                    g_loc(m, j)[...] = n_buf[both, chunk(j)]
                for i in range(1, chips):
                    g_send(m, i).start()
        mean_a, mean_ax, mean_b, mean_bx, mean_bw = (row_mean(value, inv) for value in sums)
        beta = -rinv * mean_ax - square * (mean_bw - 3.0 * mean_bx * slope)
        gamma = -square * mean_bx
        alpha = lean * mean_b - rinv * mean_a
        values = (
            alpha - beta * rinv * mean_u - gamma * mean_w,
            beta * rinv,
            gamma,
            -rinv * mean_b - gamma * mean_u,
            gamma,
            1.0,
            jnp.where(s == last, jnp.sum(moved, axis=1, keepdims=True), told),
        )
        packed = 0.0
        for at, value in enumerate(values):
            packed = jnp.where(lane == at, value, packed)
        rs_out[m] = packed
        scalar_send(m).start()
        g_all[m, chip] = own_block(m)
        return carry

    def own_block(m):
        cols = pl.ds(pl.multiple_of(my_col * cw, cw), cw)
        return w_vm[pl.ds(pl.multiple_of(pitch + m * pair, pair), pair), cols]

    lax.fori_loop(0, micros, backward, 0)

    base = 2 * pitch
    depth = chips * pair

    def n_load(m):
        return pltpu.make_async_copy(
            n_hbm.at[m], w_vm.at[pl.ds(base + m * depth, depth), pl.ds(0, ncols)], load_sem.at[m]
        )

    for m in range(micros):
        n_own(m).wait()
        wait_bytes(n_hbm.at[m, pl.ds(0, depth - pair)], n_rsem.at[m])
        n_load(m).start()
    spot = base if halves > 1 else base + micros * depth
    ex_send = w_vm.at[pl.ds(spot, keep), pl.ds(feat // 2, cw)]
    fin_send = w_vm.at[pl.ds(spot, keep), pl.ds(feat // 2 + cw, cw)]
    most = micros * 3 // 4

    def block(start, first, count):
        cols = pl.ds(pl.multiple_of(start, 128), tile)
        left = w_vm[pl.ds(base + first * depth, count * depth), cols]
        right = g_all[pl.ds(first, count)].reshape(count * depth, cw)
        return lax.dot_general(left, right, (((0,), (0,)), ((), ())), preferred_element_type=F32)

    def gathered(first, count):
        for m in range(first, first + count):
            wait_bytes(g_all.at[m, pl.ds(0, chips - 1)], g_rsem.at[m])
            n_load(m).wait()

    starts = [(1 - core) * keep, (1 - core) * keep + tile, core * keep, core * keep + tile]
    gathered(0, most)
    for i in range(4):
        grad_acc[i] = block(starts[i], 0, most)
    gathered(most, micros - most)

    def ex_copy(i):
        at = pl.ds(i * tile, tile)
        return pltpu.make_async_remote_copy(
            src_ref=ex_send.at[at],
            dst_ref=ex_recv.at[at],
            send_sem=e_ssem.at[i],
            recv_sem=e_rsem.at[i],
            device_id=(s, d + 1 - 2 * core),
            device_id_type=MESH,
        )

    goal = (2 * my_half + core) * 4
    grad_cols = pl.ds(pl.multiple_of(my_col * cw, cw), cw)

    def piece_send(j):
        return pltpu.make_async_remote_copy(
            src_ref=fin_send.at[pl.ds(j * piece, piece)],
            dst_ref=grad_out.at[:, grad_cols],
            send_sem=f_ssem.at[j],
            recv_sem=f_rsem.at[my_col],
            device_id=(s, goal + j),
            device_id_type=MESH,
        )

    def piece_own(j):
        return pltpu.make_async_copy(
            fin_send.at[pl.ds(j * piece, piece)], grad_out.at[:, grad_cols], f_rsem.at[my_col]
        )

    for i in range(2):
        ex_send[pl.ds(i * tile, tile), :] = (
            grad_acc[i] + block(starts[i], most, micros - most)
        ).astype(BF16)
        ex_copy(i).start()
    for i in range(2):
        at = pl.ds(i * tile, tile)
        mine = grad_acc[2 + i] + block(starts[2 + i], most, micros - most)
        wait_bytes(ex_recv.at[at], e_rsem.at[i])
        fin_send[at, :] = (mine + ex_recv[at, :].astype(F32)).astype(BF16)
        for j in (2 * i, 2 * i + 1):

            @pl.when(goal + j != d)
            def _():
                piece_send(j).start()

            @pl.when(goal + j == d)
            def _():
                piece_own(j).start()

    for copy in own_copies:
        copy.wait()
    for k in range(CHUNKS):
        wait_bytes(x_in.at[spare, k, top], x_rsem.at[spare, k])
        wait_bytes(c_in.at[spare, k, top], c_rsem.at[spare, k])
    wait_bytes(rs_in.at[spare], rs_rsem.at[spare])
    step = step_ref[...]
    scalars = jnp.where(s == 0, rs_out[0], rs_in[spare])
    for k in range(CHUNKS):
        sign = own_sign[:, chunk(k)].astype(F32)
        start = own_state[:, chunk(k)].astype(F32)
        first = own_adjoint[:, chunk(k)].astype(F32)
        final_u = x_in[spare, k, top, :].astype(F32)
        state_out[:, chunk(k)] = start - step * (final_u - start)
        back = jnp.where(s == 0, c_out(0, k)[top, :].astype(F32), c_in[spare, k, top, :].astype(F32))
        back = back + (scalars[:, 0:1] + scalars[:, 1:2] * start + scalars[:, 2:3] * sign)
        adjoint_out[:, chunk(k)] = first + step * (back - first)
    summed = jnp.sum(scalars[:, 6:7], axis=0, keepdims=True)
    which = lax.broadcasted_iota(jnp.int32, (1, micros), 1)
    mine = jnp.sum(jnp.where(which == s, logp_ref[...], 0.0), axis=1, keepdims=True)
    logp_out[...] = mine + step * (summed / (tok * feat))

    def drain(m, carry):
        wait_bytes(n_hbm.at[m, pl.ds(0, depth - pair)], n_ssem.at[m])
        wait_bytes(g_all.at[m, pl.ds(0, chips - 1)], g_ssem.at[m])
        scalar_send(m).wait_send()

        @pl.when(s < last)
        def _():
            for k in range(CHUNKS):
                wait_bytes(out_buf.at[m, k], x_ssem.at[m, k])

        @pl.when(s == last)
        def _():
            for k in range(CHUNKS):
                wait_bytes(out_buf.at[m, k, top], x_ssem.at[m, k])

        @pl.when(s > 0)
        def _():
            for k in range(CHUNKS):
                wait_bytes(c_in.at[m, k], c_ssem.at[m, k])

        @pl.when(s == 0)
        def _():
            for k in range(CHUNKS):
                wait_bytes(c_in.at[m, k, top], c_ssem.at[m, k])

        return carry

    lax.fori_loop(0, micros, drain, 0)
    for i in range(2):
        ex_copy(i).wait_send()
    for j in range(4):

        @pl.when(goal + j != d)
        def _():
            piece_send(j).wait_send()

        wait_bytes(grad_out.at[:, chunk(j)], f_rsem.at[j])


def run_kernel(sections, dp_size, tok, feat, *operands):
    micros = sections
    cw = feat // CHUNKS
    pair = 2 * tok
    chips = dp_size // 2
    halves = chips // 4
    ncols = feat // halves
    keep = ncols // 2
    piece = keep // 4
    dma = pltpu.SemaphoreType.DMA
    anywhere = pl.BlockSpec(memory_space=pl.ANY)
    vmem = pl.BlockSpec(memory_space=pltpu.VMEM)
    return pl.pallas_call(
        functools.partial(kernel, sections, dp_size, tok, feat),
        out_shape=(
            jax.ShapeDtypeStruct((tok, feat), F32),
            jax.ShapeDtypeStruct((tok, feat), F32),
            jax.ShapeDtypeStruct((1, 1), F32),
            jax.ShapeDtypeStruct((piece, feat), BF16),
            jax.ShapeDtypeStruct((micros, chips * pair, ncols), BF16),
        ),
        in_specs=[anywhere] * 3 + [vmem] * 6 + [anywhere],
        out_specs=(vmem, vmem, vmem, anywhere, anywhere),
        scratch_shapes=[
            pltpu.VMEM((feat, feat), BF16),
            pltpu.VMEM((feat, feat), BF16),
            pltpu.VMEM((micros + 1, CHUNKS, pair, cw), BF16),
            pltpu.VMEM((micros, CHUNKS, pair, cw), BF16),
            pltpu.VMEM((micros + 1, CHUNKS, pair, cw), BF16),
            pltpu.VMEM((LHS_ROWS, feat), BF16),
            pltpu.VMEM((micros, halves, pair, ncols), BF16),
            pltpu.VMEM((micros, chips, pair, cw), BF16),
            pltpu.VMEM((micros, CHUNKS, tok, cw), F32),
            pltpu.VMEM((micros, CHUNKS, tok, cw), F32),
            pltpu.VMEM((CHUNKS, pair, cw), F32),
            pltpu.VMEM((micros, 4, tok, 128), F32),
            pltpu.VMEM((micros + 1, tok, 128), F32),
            pltpu.VMEM((micros, tok, 128), F32),
            pltpu.VMEM((micros, tok, feat), jnp.int32),
            pltpu.VMEM((tok, feat), jnp.int32),
            pltpu.VMEM((tok, feat), BF16),
            pltpu.VMEM((tok, feat), BF16),
            pltpu.VMEM((keep, cw), BF16),
            pltpu.VMEM((4, keep // 2, cw), F32),
            dma((CHUNKS,)),
            dma((micros, CHUNKS)),
            dma((micros,)),
            dma((3,)),
            dma((micros, CHUNKS)),
            dma((micros + 1, CHUNKS)),
            dma((micros, CHUNKS)),
            dma((micros + 1, CHUNKS)),
            dma((micros,)),
            dma((micros + 1,)),
            dma((micros,)),
            dma((micros,)),
            dma((micros,)),
            dma((micros,)),
            dma((micros,)),
            dma((2,)),
            dma((2,)),
            dma((4,)),
            dma((4,)),
        ],
        compiler_params=pltpu.CompilerParams(
            collective_id=0, has_side_effects=True, vmem_limit_bytes=63 * 2**20
        ),
    )(*operands)


def body(
    state,
    adjoint,
    probe,
    logp,
    density_weight,
    step_size,
    norm_gain,
    norm_shift,
    branch_gate,
    weights,
):
    _, tok, feat = state.shape
    state_next, adjoint_next, logp_next, grad, _ = run_kernel(
        lax.axis_size("section"),
        lax.axis_size("dp"),
        tok,
        feat,
        state,
        adjoint,
        probe,
        logp.reshape(1, -1),
        density_weight.reshape(1, -1),
        step_size[None],
        norm_gain,
        norm_shift,
        branch_gate,
        weights[0],
    )
    return (state_next[None], adjoint_next[None], logp_next, grad[None].astype(F32))


def solution(mesh):
    placed = (
        P(None, "dp", None),
        P(None, "dp", None),
        P(None, "dp", None),
        P(None, "dp"),
        P(None, "dp"),
        P(),
        P("section", None),
        P("section", None),
        P("section", None),
        P("section", None, None),
    )
    return jax.shard_map(
        body,
        mesh=mesh,
        in_specs=placed,
        out_specs=(
            P("section", "dp", None),
            P("section", "dp", None),
            P("section", "dp"),
            P("section", "dp", None),
        ),
        check_vma=False,
    )
```

```python
import functools

import jax
import jax.numpy as jnp
from jax import lax
from jax.experimental import pallas as pl
from jax.experimental.pallas import tpu as pltpu
from jax.sharding import PartitionSpec as P

EPSILON = 1e-06
MESH = pl.DeviceIdType.MESH
CHUNKS = 4
LHS_ROWS = 128
ROOT_HALF = 0.7071067811865476
PHI_SCALE = 0.3989422804014327
F32 = jnp.float32
BF16 = jnp.bfloat16


def wait_bytes(ref, sem):
    pltpu.make_async_copy(ref, ref, sem).wait()


def lanes(value):
    total = value[:, 0:128]
    for at in range(128, value.shape[1], 128):
        total = total + value[:, at : at + 128]
    return total


def row_mean(value, inv):
    return jnp.sum(value, axis=1, keepdims=True) * inv


def kernel(
    sections, dp_size, tok, feat,
    state_hbm, adjoint_hbm, probe_hbm, logp_ref, dw_ref, step_ref, gain_ref, shift_ref, gate_ref, w_hbm,
    state_out, adjoint_out, logp_out, grad_out, n_hbm,
    w_vm, wt_vm, x_in, out_buf, c_in, n_buf, n_loc, g_all,
    g1_buf, g2_buf, c_buf, stats, rs_in, rs_out, signs, own_sign, own_state, own_adjoint, ex_recv, grad_acc,
    w_sem, in_sem, sign_sem, own_sem, x_ssem, x_rsem, c_ssem, c_rsem, rs_ssem, rs_rsem,
    n_ssem, n_rsem, g_ssem, g_rsem, load_sem, e_ssem, e_rsem, f_ssem, f_rsem,
):
    micros = sections
    cw = feat // CHUNKS
    pair = 2 * tok
    chips = dp_size // 2
    halves = chips // 4
    ncols = feat // halves
    keep = ncols // 2
    piece = keep // 4
    tile = keep // 2
    block_side = 256
    inv = 1.0 / feat
    half_section = sections // 2
    last = sections - 1
    spare = micros

    s = lax.axis_index("section")
    d = lax.axis_index("dp")
    core = lax.rem(d, 2)
    chip = lax.div(d, 2)
    x_at = lax.rem(chip, 2)
    d_flip = d + 2 - 4 * x_at + 1 - 2 * core
    my_half = lax.div(chip, 4)
    my_col = lax.rem(chip, 4)
    next_d = jnp.where(s == half_section - 1, d_flip, d)
    prev_d = jnp.where(s == half_section, d_flip, d)

    def chunk(k):
        return pl.ds(k * cw, cw)

    top = pl.ds(0, tok)
    low = pl.ds(tok, tok)
    both = pl.ds(0, pair)
    early = 256 if cw == 768 else 128
    parts = [(0, 0, early), (0, early, cw - early)] + [(k, 0, cw) for k in range(1, CHUNKS)]

    def w_copy(k):
        return pltpu.make_async_copy(w_hbm.at[:, chunk(k)], w_vm.at[:, chunk(k)], w_sem.at[k])

    def sign_copy(m):
        return pltpu.make_async_copy(probe_hbm.at[m], signs.at[m], sign_sem.at[m])

    def state_copy(m, k):
        return pltpu.make_async_copy(
            state_hbm.at[m, :, chunk(k)], x_in.at[m, k, top], in_sem.at[m, k]
        )

    own_copies = (
        pltpu.make_async_copy(state_hbm.at[s], own_state, own_sem.at[0]),
        pltpu.make_async_copy(adjoint_hbm.at[s], own_adjoint, own_sem.at[1]),
        pltpu.make_async_copy(probe_hbm.at[s], own_sign, own_sem.at[2]),
    )
    edge = (s == 0) | (s == last)

    @pl.when(edge)
    def _():
        for m in range(micros):
            sign_copy(m).start()

    @pl.when(s == 0)
    def _():
        for m in range(micros):
            for k in range(CHUNKS):
                state_copy(m, k).start()

    for k in range(CHUNKS):
        w_copy(k).start()
    for copy in own_copies:
        copy.start()
    n_buf[...] = jnp.zeros_like(n_buf)

    barrier = pltpu.get_barrier_semaphore()

    def greet_group(i, carry):
        other = lax.rem(d + i, dp_size)
        pl.semaphore_signal(barrier, inc=1, device_id=(s, other), device_id_type=MESH)
        return carry

    def greet_sections(i, carry):
        other = lax.rem(s + i, sections)
        pl.semaphore_signal(barrier, inc=1, device_id=(other, d), device_id_type=MESH)
        pl.semaphore_signal(barrier, inc=1, device_id=(other, d_flip), device_id_type=MESH)
        return carry

    lax.fori_loop(1, dp_size, greet_group, 0)
    lax.fori_loop(1, sections, greet_sections, 0)

    @pl.when(s == 0)
    def _():
        for m in range(micros):
            sign_copy(m).wait()
            for k in range(CHUNKS):
                x_in[m, k, low, :] = signs[m, :, chunk(k)].astype(BF16)

    @pl.when(s == last)
    def _():
        for m in range(micros):
            sign_copy(m).wait()
            for k in range(CHUNKS):
                out_buf[m, k, low, :] = signs[m, :, chunk(k)].astype(BF16)

    pl.semaphore_wait(barrier, dp_size - 1 + 2 * (sections - 1))

    lane = lax.broadcasted_iota(jnp.int32, (tok, 128), 1)

    def seed_copy(src, m, k, where):
        return pltpu.make_async_remote_copy(
            src_ref=src,
            dst_ref=c_in.at[m, k, where],
            send_sem=c_ssem.at[m, k],
            recv_sem=c_rsem.at[m, k],
            device_id=(s, d_flip),
            device_id_type=MESH,
        )

    def scalar_seed(m):
        return pltpu.make_async_remote_copy(
            src_ref=rs_out.at[m],
            dst_ref=rs_in.at[m],
            send_sem=rs_ssem.at[m],
            recv_sem=rs_rsem.at[m],
            device_id=(s, d_flip),
            device_id_type=MESH,
        )

    @pl.when(s == last)
    def _():
        for m in range(micros):
            weight = jnp.broadcast_to(dw_ref[0:1, m : m + 1], (tok, 128))
            rs_out[m] = jnp.where(lane == 5, -weight, 0.0)
            scalar_seed(m).start()
            for k in range(CHUNKS):
                seed_copy(adjoint_hbm.at[m, :, chunk(k)], m, k, top).start()
                seed_copy(out_buf.at[m, k, low], m, k, low).start()

    def transpose_weights():
        count = feat // block_side

        def one(i, carry):
            at_row = pl.multiple_of(lax.div(i, count) * block_side, block_side)
            at_col = pl.multiple_of(lax.rem(i, count) * block_side, block_side)
            wt_vm[pl.ds(at_col, block_side), pl.ds(at_row, block_side)] = w_vm[
                pl.ds(at_row, block_side), pl.ds(at_col, block_side)
            ].T
            return carry

        lax.fori_loop(0, count * count, one, 0)

    @pl.when(s >= half_section)
    def _():
        for k in range(CHUNKS):
            w_copy(k).wait()
        transpose_weights()

    @pl.when(s == last)
    def _():
        for m in range(micros):
            scalar_seed(m).wait_send()
            for k in range(CHUNKS):
                wait_bytes(out_buf.at[m, k], c_ssem.at[m, k])

    def x_send(m, k, at, width):
        cols = pl.ds(at, width)
        return pltpu.make_async_remote_copy(
            src_ref=out_buf.at[m, k, both, cols],
            dst_ref=x_in.at[m, k, both, cols],
            send_sem=x_ssem.at[m, k],
            recv_sem=x_rsem.at[m, k],
            device_id=(s + 1, next_d),
            device_id_type=MESH,
        )

    def top_send(m, k, at, width):
        cols = pl.ds(at, width)
        return pltpu.make_async_remote_copy(
            src_ref=out_buf.at[m, k, top, cols],
            dst_ref=x_in.at[spare, k, top, cols],
            send_sem=x_ssem.at[m, k],
            recv_sem=x_rsem.at[spare, k],
            device_id=(m, d_flip),
            device_id_type=MESH,
        )

    def n_send(m, i):
        other = lax.rem(chip + i, chips)
        return pltpu.make_async_remote_copy(
            src_ref=n_loc.at[m, lax.div(other, 4)],
            dst_ref=n_hbm.at[m, pl.ds(chip * pair, pair)],
            send_sem=n_ssem.at[m],
            recv_sem=n_rsem.at[m],
            device_id=(s, other * 2 + core),
            device_id_type=MESH,
        )

    def n_own(m):
        return pltpu.make_async_copy(
            n_loc.at[m, my_half], n_hbm.at[m, pl.ds(chip * pair, pair)], load_sem.at[m]
        )

    def forward(m, carry):
        def rows(k):
            return x_in[m, k, top, :].astype(F32)

        def tangents(k):
            return x_in[m, k, low, :].astype(F32)

        total_u = total_w = square = cross = 0.0
        for k in range(CHUNKS):

            @pl.when(s > 0)
            def _():
                wait_bytes(x_in.at[m, k], x_rsem.at[m, k])

            u = rows(k)
            w = tangents(k)
            if k == 0:
                base_u = row_mean(lanes(u), 1.0 / cw)
                base_w = row_mean(lanes(w), 1.0 / cw)
            u = u - base_u
            w = w - base_w
            total_u = total_u + lanes(u)
            total_w = total_w + lanes(w)
            square = square + lanes(u * u)
            cross = cross + lanes(u * w)
        shift_u = row_mean(total_u, inv)
        shift_w = row_mean(total_w, inv)
        var = row_mean(square, inv) - shift_u * shift_u
        cov = row_mean(cross, inv) - shift_u * shift_w
        mean_u = base_u + shift_u
        mean_w = base_w + shift_w
        rinv = lax.rsqrt(jnp.maximum(var, 0.0) + EPSILON)
        slope = rinv * cov
        for at, value in enumerate((mean_u, mean_w, rinv, slope)):
            stats[m, at] = jnp.broadcast_to(value, (tok, 128))
        for k in range(CHUNKS):
            gain = gain_ref[:, chunk(k)]
            xhat = (rows(k) - mean_u) * rinv
            normed = xhat * gain + shift_ref[:, chunk(k)]
            normed_t = rinv * ((tangents(k) - mean_w) - xhat * slope) * gain
            n_buf[top, chunk(k)] = normed.astype(BF16)
            n_buf[low, chunk(k)] = normed_t.astype(BF16)

        for k, at, width in parts:
            cols = pl.ds(at, width)
            wide = pl.ds(k * cw + at, width)
            if at == 0:

                @pl.when((m == 0) & (s < half_section))
                def _():
                    w_copy(k).wait()

            product = jnp.dot(n_buf[...], w_vm[:, wide], preferred_element_type=F32)
            z = product[:tok]
            z_t = product[tok:pair]
            gate = gate_ref[:, wide]
            cdf = 0.5 + 0.5 * lax.erf(z * ROOT_HALF)
            zz = z * z
            pdf = PHI_SCALE * jnp.exp(-0.5 * zz)
            first = gate * (cdf + z * pdf)
            u = x_in[m, k, top, cols].astype(F32)
            w = x_in[m, k, low, cols].astype(F32)
            out_buf[m, k, top, cols] = (u + gate * (z * cdf)).astype(BF16)
            out_buf[m, k, low, cols] = (w + first * z_t).astype(BF16)

            @pl.when(s < last)
            def _():
                x_send(m, k, at, width).start()

            @pl.when(s == last)
            def _():
                top_send(m, k, at, width).start()

            g1_buf[m, k, :, cols] = first
            g2_buf[m, k, :, cols] = gate * (pdf * (2.0 - zz)) * z_t
            if k == 0 and at == 0:
                for half in range(halves):
                    n_loc[m, half] = n_buf[both, pl.ds(half * ncols, ncols)]
                for i in range(1, chips):
                    n_send(m, i).start()
                n_own(m).start()
        return carry

    @pl.when(s == 0)
    def _():
        for m in range(micros):
            for k in range(CHUNKS):
                state_copy(m, k).wait()

    lax.fori_loop(0, micros, forward, 0)

    @pl.when(s < half_section)
    def _():
        transpose_weights()

    pitch = micros * pair

    def c_out(m, k):
        return w_vm.at[pl.ds(pl.multiple_of(m * pair, pair), pair), chunk(k)]

    def g_loc(m, k):
        return w_vm.at[pl.ds(pl.multiple_of(pitch + m * pair, pair), pair), chunk(k)]

    def c_send(m, k, at, width):
        return pltpu.make_async_remote_copy(
            src_ref=c_out(m, k).at[both, pl.ds(at, width)],
            dst_ref=c_in.at[m, k, both, pl.ds(at, width)],
            send_sem=c_ssem.at[m, k],
            recv_sem=c_rsem.at[m, k],
            device_id=(s - 1, prev_d),
            device_id_type=MESH,
        )

    def back_send(m, k, at, width):
        return pltpu.make_async_remote_copy(
            src_ref=c_out(m, k).at[top, pl.ds(at, width)],
            dst_ref=c_in.at[spare, k, top, pl.ds(at, width)],
            send_sem=c_ssem.at[m, k],
            recv_sem=c_rsem.at[spare, k],
            device_id=(m, jnp.where(m == 0, d_flip, d)),
            device_id_type=MESH,
        )

    def scalar_send(m):
        slot = jnp.where(s == 0, spare, m)
        return pltpu.make_async_remote_copy(
            src_ref=rs_out.at[m],
            dst_ref=rs_in.at[slot],
            send_sem=rs_ssem.at[m],
            recv_sem=rs_rsem.at[slot],
            device_id=(
                jnp.where(s == 0, m, s - 1),
                jnp.where((s == 0) & (m == 0), d_flip, prev_d),
            ),
            device_id_type=MESH,
        )

    def g_send(m, i):
        other = lax.rem(chip + i, chips)
        cols = pl.ds(pl.multiple_of(lax.rem(other, 4) * cw, cw), cw)
        return pltpu.make_async_remote_copy(
            src_ref=w_vm.at[pl.ds(pl.multiple_of(pitch + m * pair, pair), pair), cols],
            dst_ref=g_all.at[m, chip],
            send_sem=g_ssem.at[m],
            recv_sem=g_rsem.at[m],
            device_id=(s, other * 2 + core),
            device_id_type=MESH,
        )

    def backward(m, carry):
        for k in range(CHUNKS):
            wait_bytes(c_in.at[m, k], c_rsem.at[m, k])
        wait_bytes(rs_in.at[m], rs_rsem.at[m])
        scalars = rs_in[m]
        add_u, by_u, by_w, add_t, by_t, factor, told = (scalars[:, i : i + 1] for i in range(7))
        moved = 0.0
        for k in range(CHUNKS):
            u = out_buf[m, k, top, :].astype(F32)
            w = out_buf[m, k, low, :].astype(F32)
            c = c_in[m, k, top, :].astype(F32) + (add_u + by_u * u + by_w * w)
            sign = c_in[m, k, low, :].astype(F32)
            moved = moved + lanes(sign * (w - sign))
            c_t = sign * factor + (add_t + by_t * u)
            c_buf[k, top, :] = c
            c_buf[k, low, :] = c_t
            first = g1_buf[m, k]
            n_buf[top, chunk(k)] = (c * first + c_t * g2_buf[m, k]).astype(BF16)
            n_buf[low, chunk(k)] = (c_t * first).astype(BF16)

        mean_u = stats[m, 0][:, 0:1]
        mean_w = stats[m, 1][:, 0:1]
        rinv = stats[m, 2][:, 0:1]
        slope = stats[m, 3][:, 0:1]
        square = rinv * rinv
        lean = square * slope

        sums = [0.0] * 5
        for k, at, width in parts:
            cols = pl.ds(at, width)
            wide = pl.ds(k * cw + at, width)
            product = jnp.dot(n_buf[...], wt_vm[:, wide], preferred_element_type=F32)
            gain = gain_ref[:, wide]
            a = product[:tok] * gain
            b = product[tok:pair] * gain
            out = c_out(m, k)
            out[top, cols] = (c_buf[k, top, cols] + rinv * a - lean * b).astype(BF16)
            out[low, cols] = (c_buf[k, low, cols] + rinv * b).astype(BF16)

            @pl.when(s > 0)
            def _():
                c_send(m, k, at, width).start()

            @pl.when(s == 0)
            def _():
                back_send(m, k, at, width).start()

            xhat = (x_in[m, k, top, cols].astype(F32) - mean_u) * rinv
            centered = x_in[m, k, low, cols].astype(F32) - mean_w
            for i, value in enumerate((a, a * xhat, b, b * xhat, b * centered)):
                sums[i] = sums[i] + lanes(value)
            if k == 0 and at == 0:
                for j in range(CHUNKS):
                    g_loc(m, j)[...] = n_buf[both, chunk(j)]
                for i in range(1, chips):
                    g_send(m, i).start()
        mean_a, mean_ax, mean_b, mean_bx, mean_bw = (row_mean(value, inv) for value in sums)
        beta = -rinv * mean_ax - square * (mean_bw - 3.0 * mean_bx * slope)
        gamma = -square * mean_bx
        alpha = lean * mean_b - rinv * mean_a
        values = (
            alpha - beta * rinv * mean_u - gamma * mean_w,
            beta * rinv,
            gamma,
            -rinv * mean_b - gamma * mean_u,
            gamma,
            1.0,
            jnp.where(s == last, jnp.sum(moved, axis=1, keepdims=True), told),
        )
        packed = 0.0
        for at, value in enumerate(values):
            packed = jnp.where(lane == at, value, packed)
        rs_out[m] = packed
        scalar_send(m).start()
        g_all[m, chip] = own_block(m)
        return carry

    def own_block(m):
        cols = pl.ds(pl.multiple_of(my_col * cw, cw), cw)
        return w_vm[pl.ds(pl.multiple_of(pitch + m * pair, pair), pair), cols]

    lax.fori_loop(0, micros, backward, 0)

    base = 2 * pitch
    depth = chips * pair

    def n_load(m):
        return pltpu.make_async_copy(
            n_hbm.at[m], w_vm.at[pl.ds(base + m * depth, depth), pl.ds(0, ncols)], load_sem.at[m]
        )

    for m in range(micros):
        n_own(m).wait()
        wait_bytes(n_hbm.at[m, pl.ds(0, depth - pair)], n_rsem.at[m])
        n_load(m).start()
    spot = base if halves > 1 else base + micros * depth
    ex_send = w_vm.at[pl.ds(spot, keep), pl.ds(feat // 2, cw)]
    fin_send = w_vm.at[pl.ds(spot, keep), pl.ds(feat // 2 + cw, cw)]
    most = micros - 1

    def block(start, first, count):
        cols = pl.ds(pl.multiple_of(start, 128), tile)
        left = w_vm[pl.ds(base + first * depth, count * depth), cols]
        right = g_all[pl.ds(first, count)].reshape(count * depth, cw)
        return lax.dot_general(left, right, (((0,), (0,)), ((), ())), preferred_element_type=F32)

    def gathered(first, count):
        for m in range(first, first + count):
            wait_bytes(g_all.at[m, pl.ds(0, chips - 1)], g_rsem.at[m])
            n_load(m).wait()

    starts = [(1 - core) * keep, (1 - core) * keep + tile, core * keep, core * keep + tile]
    gathered(0, most)
    for i in range(4):
        grad_acc[i] = block(starts[i], 0, most)
    gathered(most, micros - most)

    def ex_copy(i):
        at = pl.ds(pl.multiple_of(i * tile, tile), tile)
        return pltpu.make_async_remote_copy(
            src_ref=ex_send.at[at],
            dst_ref=ex_recv.at[at],
            send_sem=e_ssem.at[i],
            recv_sem=e_rsem.at[i],
            device_id=(s, d + 1 - 2 * core),
            device_id_type=MESH,
        )

    goal = (2 * my_half + core) * 4
    grad_cols = pl.ds(pl.multiple_of(my_col * cw, cw), cw)

    def piece_send(j):
        return pltpu.make_async_remote_copy(
            src_ref=fin_send.at[pl.ds(pl.multiple_of(j * piece, 16), piece)],
            dst_ref=grad_out.at[:, grad_cols],
            send_sem=f_ssem.at[j],
            recv_sem=f_rsem.at[my_col],
            device_id=(s, goal + j),
            device_id_type=MESH,
        )

    def piece_own(j):
        return pltpu.make_async_copy(
            fin_send.at[pl.ds(pl.multiple_of(j * piece, 16), piece)], grad_out.at[:, grad_cols], f_rsem.at[my_col]
        )

    order = (1 - x_at, x_at)

    for t in order:
        late = block((1 - core) * keep + t * tile, most, micros - most)
        at = pl.ds(pl.multiple_of(t * tile, tile), tile)
        ex_send[at, :] = (grad_acc[t] + late).astype(BF16)
        ex_copy(t).start()
    for t in order:
        at = pl.ds(pl.multiple_of(t * tile, tile), tile)
        mine = grad_acc[2 + t] + block(core * keep + t * tile, most, micros - most)
        wait_bytes(ex_recv.at[at], e_rsem.at[t])
        fin_send[at, :] = (mine + ex_recv[at, :].astype(F32)).astype(BF16)
        for j in (2 * t, 2 * t + 1):

            @pl.when(goal + j != d)
            def _():
                piece_send(j).start()

            @pl.when(goal + j == d)
            def _():
                piece_own(j).start()

    for copy in own_copies:
        copy.wait()
    for k in range(CHUNKS):
        wait_bytes(x_in.at[spare, k, top], x_rsem.at[spare, k])
        wait_bytes(c_in.at[spare, k, top], c_rsem.at[spare, k])
    wait_bytes(rs_in.at[spare], rs_rsem.at[spare])
    step = step_ref[...]
    scalars = jnp.where(s == 0, rs_out[0], rs_in[spare])
    for k in range(CHUNKS):
        sign = own_sign[:, chunk(k)].astype(F32)
        start = own_state[:, chunk(k)].astype(F32)
        first = own_adjoint[:, chunk(k)].astype(F32)
        final_u = x_in[spare, k, top, :].astype(F32)
        state_out[:, chunk(k)] = start - step * (final_u - start)
        back = jnp.where(s == 0, c_out(0, k)[top, :].astype(F32), c_in[spare, k, top, :].astype(F32))
        back = back + (scalars[:, 0:1] + scalars[:, 1:2] * start + scalars[:, 2:3] * sign)
        adjoint_out[:, chunk(k)] = first + step * (back - first)
    summed = jnp.sum(scalars[:, 6:7], axis=0, keepdims=True)
    which = lax.broadcasted_iota(jnp.int32, (1, micros), 1)
    mine = jnp.sum(jnp.where(which == s, logp_ref[...], 0.0), axis=1, keepdims=True)
    logp_out[...] = mine + step * (summed / (tok * feat))

    def drain(m, carry):
        wait_bytes(n_hbm.at[m, pl.ds(0, depth - pair)], n_ssem.at[m])
        wait_bytes(g_all.at[m, pl.ds(0, chips - 1)], g_ssem.at[m])
        scalar_send(m).wait_send()

        @pl.when(s < last)
        def _():
            for k in range(CHUNKS):
                wait_bytes(out_buf.at[m, k], x_ssem.at[m, k])

        @pl.when(s == last)
        def _():
            for k in range(CHUNKS):
                wait_bytes(out_buf.at[m, k, top], x_ssem.at[m, k])

        @pl.when(s > 0)
        def _():
            for k in range(CHUNKS):
                wait_bytes(c_in.at[m, k], c_ssem.at[m, k])

        @pl.when(s == 0)
        def _():
            for k in range(CHUNKS):
                wait_bytes(c_in.at[m, k, top], c_ssem.at[m, k])

        return carry

    lax.fori_loop(0, micros, drain, 0)
    for i in range(2):
        ex_copy(i).wait_send()
    for j in range(4):

        @pl.when(goal + j != d)
        def _():
            piece_send(j).wait_send()

        wait_bytes(grad_out.at[:, chunk(j)], f_rsem.at[j])


def run_kernel(sections, dp_size, tok, feat, *operands):
    micros = sections
    cw = feat // CHUNKS
    pair = 2 * tok
    chips = dp_size // 2
    halves = chips // 4
    ncols = feat // halves
    keep = ncols // 2
    piece = keep // 4
    dma = pltpu.SemaphoreType.DMA
    anywhere = pl.BlockSpec(memory_space=pl.ANY)
    vmem = pl.BlockSpec(memory_space=pltpu.VMEM)
    return pl.pallas_call(
        functools.partial(kernel, sections, dp_size, tok, feat),
        out_shape=(
            jax.ShapeDtypeStruct((tok, feat), F32),
            jax.ShapeDtypeStruct((tok, feat), F32),
            jax.ShapeDtypeStruct((1, 1), F32),
            jax.ShapeDtypeStruct((piece, feat), BF16),
            jax.ShapeDtypeStruct((micros, chips * pair, ncols), BF16),
        ),
        in_specs=[anywhere] * 3 + [vmem] * 6 + [anywhere],
        out_specs=(vmem, vmem, vmem, anywhere, anywhere),
        scratch_shapes=[
            pltpu.VMEM((feat, feat), BF16),
            pltpu.VMEM((feat, feat), BF16),
            pltpu.VMEM((micros + 1, CHUNKS, pair, cw), BF16),
            pltpu.VMEM((micros, CHUNKS, pair, cw), BF16),
            pltpu.VMEM((micros + 1, CHUNKS, pair, cw), BF16),
            pltpu.VMEM((LHS_ROWS, feat), BF16),
            pltpu.VMEM((micros, halves, pair, ncols), BF16),
            pltpu.VMEM((micros, chips, pair, cw), BF16),
            pltpu.VMEM((micros, CHUNKS, tok, cw), F32),
            pltpu.VMEM((micros, CHUNKS, tok, cw), F32),
            pltpu.VMEM((CHUNKS, pair, cw), F32),
            pltpu.VMEM((micros, 4, tok, 128), F32),
            pltpu.VMEM((micros + 1, tok, 128), F32),
            pltpu.VMEM((micros, tok, 128), F32),
            pltpu.VMEM((micros, tok, feat), jnp.int32),
            pltpu.VMEM((tok, feat), jnp.int32),
            pltpu.VMEM((tok, feat), BF16),
            pltpu.VMEM((tok, feat), BF16),
            pltpu.VMEM((keep, cw), BF16),
            pltpu.VMEM((4, keep // 2, cw), F32),
            dma((CHUNKS,)),
            dma((micros, CHUNKS)),
            dma((micros,)),
            dma((3,)),
            dma((micros, CHUNKS)),
            dma((micros + 1, CHUNKS)),
            dma((micros, CHUNKS)),
            dma((micros + 1, CHUNKS)),
            dma((micros,)),
            dma((micros + 1,)),
            dma((micros,)),
            dma((micros,)),
            dma((micros,)),
            dma((micros,)),
            dma((micros,)),
            dma((2,)),
            dma((2,)),
            dma((4,)),
            dma((4,)),
        ],
        compiler_params=pltpu.CompilerParams(
            collective_id=0, has_side_effects=True, vmem_limit_bytes=63 * 2**20
        ),
    )(*operands)


def body(
    state,
    adjoint,
    probe,
    logp,
    density_weight,
    step_size,
    norm_gain,
    norm_shift,
    branch_gate,
    weights,
):
    _, tok, feat = state.shape
    state_next, adjoint_next, logp_next, grad, _ = run_kernel(
        lax.axis_size("section"),
        lax.axis_size("dp"),
        tok,
        feat,
        state,
        adjoint,
        probe,
        logp.reshape(1, -1),
        density_weight.reshape(1, -1),
        step_size[None],
        norm_gain,
        norm_shift,
        branch_gate,
        weights[0],
    )
    return (state_next[None], adjoint_next[None], logp_next, grad[None].astype(F32))


def solution(mesh):
    placed = (
        P(None, "dp", None),
        P(None, "dp", None),
        P(None, "dp", None),
        P(None, "dp"),
        P(None, "dp"),
        P(),
        P("section", None),
        P("section", None),
        P("section", None),
        P("section", None, None),
    )
    return jax.shard_map(
        body,
        mesh=mesh,
        in_specs=placed,
        out_specs=(
            P("section", "dp", None),
            P("section", "dp", None),
            P("section", "dp"),
            P("section", "dp", None),
        ),
        check_vma=False,
    )
```
